32 devices in a mesh: grp: 2 (over y), orb: 16 (over z, x, core).
Axes of the slice: x: 2, y: 2, z: 4, core: 2. Of those that a mesh axis runs over, the one named last changes fastest.
Arguments:
- occupied: float32 [16, 262144], P('orb'), may hold values from -5 to 5
- targets: float32 [32, 262144], P(('grp', 'orb')), may hold values from -8 to 8
- potential: float32 [262144], P('orb'), may hold values from -4 to 4
Outputs:
- updated: float32 [32, 262144], P('grp', 'orb')
The draws below stay inside these ranges and needn't reach their ends.
All inputs are finite; a program needn't handle non-finite values.
Results may differ from the reference program's by a relative error of at most 0.0003.
Values sent between devices are 32-bit elements; how exact they have to be, the bound alone decides.
No kernel may reach another device: no remote copies, remote signals or barrier semaphores. Data moves between devices by JAX's collectives and lax.ppermute only.
A program may use at most 64 MiB of HBM per device.

```python
import jax
import jax.numpy as jnp
from jax import lax

NGRID = 64
CELLS = 262144
TGT_DEV = 1
OCC_DEV = 1
CYCLE = 2
INNER = 1
NT = 32
NOCC = 16
N_GRP = 2
N_ORB = 16


def draw_targets(key, part):
    first_key, second_key = jax.random.split(jax.random.fold_in(key, 11), 2)
    common = jnp.clip(jax.random.normal(second_key, (1, CELLS), jnp.float32), -5.0, 5.0)
    rough = jnp.clip(jax.random.normal(first_key, (NT, CELLS), jnp.float32), -5.0, 5.0)
    return rough + 0.6 * common


def levels(stream_key, shape, cuts, low, high):
    gain, own = 1.0, jax.random.fold_in(stream_key, 6)
    for dim, parts in cuts:
        heights = jnp.exp(jax.random.uniform(jax.random.fold_in(own, dim), (parts,), jnp.float32, low / len(cuts), high / len(cuts)))
        gain = gain * jnp.repeat(heights, shape[dim] // parts).reshape([-1 if axis == dim else 1 for axis in range(len(shape))])
    return gain


def scatter_about(key, dims, scale, limit, cuts=(), kind=jnp.bfloat16):
    gain = levels(key, dims, cuts, -0.22, 0.18) if cuts else 1.0
    drawn = jax.random.normal(key, dims, jnp.float32) * scale * gain
    return jnp.minimum(jnp.maximum(drawn, -limit), limit).astype(kind)


def setup_inputs(seed: int = 0) -> dict:
    seeds = jax.random.split(jax.random.key(seed), 4)
    return {
        "occupied": scatter_about(seeds[0], (NOCC, CELLS), 1.0, 5.0, ((0, 16),), jnp.float32),
        "targets": draw_targets(jax.random.fold_in(seeds[3], 71), 0),
        "potential": scatter_about(seeds[2], (CELLS,), 1.0, 4.0, ((0, 16),), jnp.float32),
    }


SCREEN_SQ = 0.04
BOX_LENGTH = 20.0
STEP_SIZE = 0.3

def kernel_cube():
    points = NGRID
    index = jnp.arange(points, dtype=jnp.int32)
    folded = jnp.minimum(index, points - index).astype(jnp.float32) * (2.0 * jnp.pi / BOX_LENGTH)
    squared = folded * folded
    total_sq = squared[:, None, None] + squared[None, :, None] + squared[None, None, :]
    return 4.0 * jnp.pi / (total_sq + SCREEN_SQ)

def coulomb_solve(fields):
    points = NGRID
    cube = fields.reshape(-1, points, points, points)
    spectrum = jnp.fft.rfftn(cube, axes=(1, 2, 3))
    kernel = kernel_cube()[:, :, :points // 2 + 1]
    solved = jnp.fft.irfftn(spectrum * kernel, s=(points, points, points), axes=(1, 2, 3))
    return solved.reshape(fields.shape)

def exchange_rows(position, occupied, targets):
    rows = lax.dynamic_slice_in_dim(targets, position * TGT_DEV, TGT_DEV, 0)
    center = position % N_ORB
    offsets = jnp.arange(-CYCLE, CYCLE + 1, dtype=jnp.int32)
    blocks = (center + offsets) % N_ORB
    row_ids = (blocks[:, None] * OCC_DEV + jnp.arange(OCC_DEV, dtype=jnp.int32)[None, :]).reshape(-1)
    nearby = jnp.take(occupied, row_ids, axis=0)
    products = (rows[:, None, :] * nearby[None, :, :]).reshape(-1, CELLS)
    solved = coulomb_solve(products).reshape(TGT_DEV, -1, CELLS)
    return -jnp.sum(nearby[None] * solved, axis=1)

def gram(left, right):
    inner = lax.dot_general(left, right, (((1,), (1,)), ((), ())), precision=lax.Precision.HIGHEST)
    return inner / CELLS

def reference(occupied, targets, potential):
    positions = jnp.arange(N_GRP * N_ORB, dtype=jnp.int32)
    exchange = lax.map(lambda position: exchange_rows(position, occupied, targets), positions).reshape(NT, CELLS)
    correlation = gram(exchange, exchange)
    factor = jnp.linalg.cholesky(correlation)
    compressed = lax.linalg.triangular_solve(factor, exchange, left_side=True, lower=True)
    current = targets
    for repeat in range(INNER):
        projection = gram(current, compressed)
        applied = potential[None, :] * current - jnp.dot(projection, compressed, precision=lax.Precision.HIGHEST)
        rayleigh = gram(applied, current)
        current = current - STEP_SIZE * (applied - jnp.dot(rayleigh, current, precision=lax.Precision.HIGHEST))
    return current
```

```python
import functools

import jax
import jax.numpy as jnp
import ml_dtypes
import numpy as np
from jax import lax
from jax.experimental import pallas as pl
from jax.experimental.pallas import tpu as pltpu
from jax.sharding import PartitionSpec as P

NGRID = 64
CELLS = 262144
LANES = 128
ROWS = CELLS // LANES
SLAB = NGRID * NGRID // LANES
CHUNK = 32
HALVES = NGRID // CHUNK

SCREEN_SQ = 0.04
BOX_LENGTH = 20.0
STEP_SIZE = 0.3

bf16 = jnp.bfloat16
f32 = jnp.float32
VMEM = pl.BlockSpec(memory_space=pltpu.VMEM)
SMEM = pl.BlockSpec(memory_space=pltpu.SMEM)


def tables():
    index = np.arange(NGRID)
    angles = 2.0 * np.pi * (index[:, None] * index[None, :] % NGRID) / NGRID
    table = np.cos(angles) + np.sin(angles)
    high = table.astype(ml_dtypes.bfloat16)
    low = (table - high.astype(np.float64)).astype(ml_dtypes.bfloat16)

    def twice(block):
        both = np.zeros((2 * NGRID, 2 * NGRID), ml_dtypes.bfloat16)
        both[:NGRID, :NGRID] = block
        both[NGRID:, NGRID:] = block
        return both

    def stacked(high, low):
        return np.concatenate([high, high, low, low], 1)

    row = np.concatenate([twice(high), twice(low)], 1)
    along_z = np.concatenate([row, row], 0)
    order = np.concatenate([index[0::2], index[1::2]])
    return (
        along_z,
        stacked(high, low),
        stacked(high[:, order], low[:, order]),
        stacked(high[order], low[order]),
    )


def halves(value):
    high = value.astype(bf16)
    return high, (value - high.astype(f32)).astype(bf16)


def dot(left, right):
    return jnp.dot(left, right, preferred_element_type=f32)


def along_lanes(value, table):
    out = dot(jnp.concatenate(halves(value), 1), table)
    return out[:, :LANES] + out[:, LANES:]


def along_rows(value, table):
    high, low = halves(value)
    return dot(table, jnp.concatenate([high, low, high, low], 0))


def beside(blocks):
    return jnp.concatenate(blocks, 1)


def apart(value):
    return [value[:, i : i + LANES] for i in range(0, value.shape[1], LANES)]


def pair_kernel(has_acc, pieces, n_grp, n_orb, flags_ref, t_ref, *refs):
    a_refs, b_refs, refs = refs[:HALVES], refs[HALVES : 2 * HALVES], refs[2 * HALVES :]
    if has_acc:
        acc_ref, refs = refs[0], refs[1:]
    z_ref, x_ref, yf_ref, yi_ref, out_ref, s_ref, s2_ref = refs
    first = lax.broadcasted_iota(jnp.int32, (1, LANES), 1) < NGRID
    rows = SLAB * CHUNK
    scale_b = flags_ref[0]

    for c in range(HALVES):
        t = t_ref[c * rows : (c + 1) * rows, :]
        pa = t * a_refs[c][...]
        pb = t * (b_refs[c][...] * scale_b)
        even = jnp.where(first, pa, pltpu.roll(pb, NGRID, 1)).reshape(CHUNK, SLAB, LANES)
        odd = jnp.where(first, pltpu.roll(pa, NGRID, 1), pb).reshape(CHUNK, SLAB, LANES)
        v = jnp.concatenate([even, odd], 1).reshape(CHUNK * NGRID, LANES)
        v = along_lanes(v, z_ref[...]).reshape(CHUNK, NGRID, LANES)
        v = along_rows(beside([v[i] for i in range(CHUNK)]), yf_ref[...])
        for i, block in enumerate(apart(v)):
            s_ref[(c * CHUNK + i) * NGRID : (c * CHUNK + i + 1) * NGRID, :] = block

    def squared(k):
        wave = jnp.minimum(k, NGRID - k).astype(f32) * (2.0 * np.pi / BOX_LENGTH)
        return wave * wave

    cube = (NGRID, LANES)
    base = (
        squared(lax.broadcasted_iota(jnp.int32, cube, 0))
        + squared(lax.broadcasted_iota(jnp.int32, cube, 1) % NGRID)
        + SCREEN_SQ
    )
    for c in range(HALVES):
        v = beside([s_ref[pl.ds(c * CHUNK + i, NGRID, stride=NGRID), :] for i in range(CHUNK)])
        v = along_rows(v, x_ref[...])
        kernel = []
        for i in range(CHUNK):
            y = c * CHUNK + i
            wave = min(y, NGRID - y) * (2.0 * np.pi / BOX_LENGTH)
            kernel.append((4.0 * np.pi / CELLS) / (base + wave * wave))
        v = along_rows(v * beside(kernel), x_ref[...])
        for i, block in enumerate(apart(v)):
            s2_ref[(c * CHUNK + i) * NGRID : (c * CHUNK + i + 1) * NGRID, :] = block

    for c in range(HALVES):
        v = beside([s2_ref[pl.ds(c * CHUNK + i, NGRID, stride=NGRID), :] for i in range(CHUNK)])
        v = jnp.concatenate(apart(along_rows(v, yi_ref[...])), 0)
        v = along_lanes(v, z_ref[...]).reshape(CHUNK, NGRID, LANES)
        even = v[:, :SLAB].reshape(rows, LANES)
        odd = v[:, SLAB:].reshape(rows, LANES)
        sa = jnp.where(first, even, pltpu.roll(odd, NGRID, 1))
        sb = jnp.where(first, pltpu.roll(even, NGRID, 1), odd)
        added = -(a_refs[c][...] * sa + (b_refs[c][...] * scale_b) * sb)
        if has_acc:
            added = acc_ref[c * rows : (c + 1) * rows, :] + added
        if pieces:
            part = ROWS // (n_grp * n_orb)
            count = n_orb // HALVES
            cut = added.reshape(count, n_grp, part, LANES)
            for g in range(n_grp):
                start = (g * n_orb + c * count) * part
                out_ref[start : start + count * part, :] = cut[:, g].reshape(count * part, LANES)
        else:
            out_ref[c * rows : (c + 1) * rows, :] = added


def pair_step(flag, target, first, second, acc, cut, n_grp, n_orb):
    args = [target, *first, *second] + ([] if acc is None else [acc])
    args += [jnp.asarray(table) for table in tables()]
    return pl.pallas_call(
        functools.partial(pair_kernel, acc is not None, cut, n_grp, n_orb),
        out_shape=jax.ShapeDtypeStruct((ROWS, LANES), f32),
        in_specs=[SMEM] + [VMEM] * len(args),
        out_specs=VMEM,
        scratch_shapes=[pltpu.VMEM((NGRID * NGRID, LANES), f32)] * 2,
        compiler_params=pltpu.CompilerParams(vmem_limit_bytes=40 << 20),
        cost_estimate=pl.CostEstimate(flops=8 * 10**9, bytes_accessed=5 << 20, transcendentals=0),
    )(flag.reshape(1), *args)


def strided(ref, r, count, step):
    return ref[pl.ds(r, count, stride=step), :]


def gram_kernel(n, part, x_ref, t_ref, v_ref, out_ref):
    x = beside([strided(x_ref, r, n, part) for r in range(part)])
    t = beside([strided(t_ref, r, n, part) for r in range(part)])
    v = beside([v_ref[r : r + 1, :] for r in range(part)])
    xh, xl = halves(x)
    th, tl = halves(t)
    wh, wl = halves(t * v)
    left = jnp.concatenate([xh, th, xl, tl], 0)
    right = jnp.concatenate([xh, th, wh, xl, tl, wl], 0)
    full = lax.dot_general(left, right, (((1,), (1,)), ((), ())), preferred_element_type=f32)
    full = full[: 2 * n] + full[2 * n :]
    full = full[:, : 3 * n] + full[:, 3 * n :]
    out_ref[...] = jnp.concatenate([full[:n, : 2 * n], full[n:, 2 * n :]], 1) * (1.0 / CELLS)


def gram_step(x, t, v, n, part):
    return pl.pallas_call(
        functools.partial(gram_kernel, n, part),
        out_shape=jax.ShapeDtypeStruct((n, 3 * n), f32),
        in_specs=[VMEM] * 3,
        out_specs=VMEM,
        compiler_params=pltpu.CompilerParams(vmem_limit_bytes=32 << 20),
        cost_estimate=pl.CostEstimate(flops=10**9, bytes_accessed=2 << 20, transcendentals=0),
    )(x, t, v)


def exact(left, right, dims):
    return lax.dot_general(
        left, right, (dims, ((), ())), precision=lax.Precision.HIGHEST, preferred_element_type=f32
    )


def update_kernel(n, part, out_rows, place_ref, g_ref, x_ref, t_ref, xo_ref, to_ref, v_ref, out_ref, m_ref, r_ref):
    group = place_ref[0]
    ids = lax.broadcasted_iota(jnp.int32, (n, 1), 0)
    columns = lax.broadcasted_iota(jnp.int32, (1, 3 * n), 1)
    eye = (lax.broadcasted_iota(jnp.int32, (n, n), 0) == lax.broadcasted_iota(jnp.int32, (n, n), 1)).astype(f32)
    work = jnp.concatenate([g_ref[:, : 2 * n], eye], 1)

    def eliminate(k, work):
        row = jnp.sum(jnp.where(ids == k, work, 0.0), axis=0, keepdims=True)
        pivot = jnp.sum(jnp.where(columns == k, row, 0.0), axis=1, keepdims=True)
        column = jnp.sum(jnp.where(columns == k, work, 0.0), axis=1, keepdims=True)
        root = lax.rsqrt(pivot)
        row = row * root
        lower = work - jnp.where(ids > k, column * root, 0.0) * row
        return jnp.where(ids == k, row, lower)

    work = lax.fori_loop(0, n, eliminate, work)
    pt = work[:, n : 2 * n]
    m_ref[...] = exact(pt, work[:, 2 * n :], ((0,), (0,)))
    r_ref[...] = g_ref[:, 2 * n :] - exact(pt, pt, ((0,), (0,)))
    start = pl.multiple_of(group * out_rows, 8)
    mix = jnp.concatenate([m_ref[pl.ds(start, out_rows), :], r_ref[pl.ds(start, out_rows), :]], 1) * STEP_SIZE
    high, low = halves(mix)
    mix = jnp.concatenate([jnp.concatenate([high, high], 1), jnp.concatenate([low, low], 1)], 0)

    def half(xs, ts, where):
        x = beside([strided(xs, r, n, part) for r in range(part)])
        t = beside([strided(ts, r, n, part) for r in range(part)])
        own = beside([ts[pl.ds(start * part + r, out_rows, stride=part), :] for r in range(part)])
        v = v_ref[pl.ds(pl.multiple_of(where * part, part), part), :]
        v = beside([v[r : r + 1] for r in range(part)])
        xh, xl = halves(x)
        th, tl = halves(t)
        both = dot(mix, jnp.concatenate([xh, th, xl, tl], 0))
        both = both[:out_rows] + both[out_rows:]
        width = part * LANES
        out_ref[:, pl.ds(pl.multiple_of(where * width, width), width)] = own * (1.0 - STEP_SIZE * v) + both

    half(x_ref, t_ref, group)
    half(xo_ref, to_ref, 1 - group)


def update_step(place, g, x, t, xo, to, v, n, part, out_rows):
    return pl.pallas_call(
        functools.partial(update_kernel, n, part, out_rows),
        out_shape=jax.ShapeDtypeStruct((out_rows, 2 * part * LANES), f32),
        in_specs=[SMEM] + [VMEM] * 6,
        out_specs=VMEM,
        scratch_shapes=[pltpu.VMEM((n, n), f32)] * 2,
        compiler_params=pltpu.CompilerParams(vmem_limit_bytes=32 << 20),
        cost_estimate=pl.CostEstimate(flops=10**9, bytes_accessed=6 << 20, transcendentals=0),
    )(place.reshape(1), g, x, t, xo, to, v)


def moved(x, axes, target):
    size = 1
    for axis in axes:
        size *= lax.axis_size(axis)
    return lax.ppermute(x, axes, [(i, target(i)) for i in range(size)])


def summed_all(x, n_grp, n_orb):
    axes = ("grp", "orb")
    bits = [1, 2, n_orb] + [b for b in (1 << k for k in range(2, 30)) if b < n_orb]
    steps = [bits[:1]] + [bits[k : k + 2] for k in range(1, len(bits), 2)]
    for step in steps:
        masks = step if len(step) == 1 else [step[0], step[1], step[0] ^ step[1]]
        parts = [moved(x, axes, lambda i, m=m: i ^ m) for m in masks]
        for part in parts:
            x = x + part
    return x


def on_device(occupied, targets, potential):
    n_grp, n_orb = lax.axis_size("grp"), lax.axis_size("orb")
    n = n_grp * n_orb
    part = ROWS // n
    group, orb = lax.axis_index("grp"), lax.axis_index("orb")
    one = jnp.ones((), f32)
    crossed = (((orb >> 1) & 1) != (orb & 1)).astype(f32)

    target = targets.reshape(ROWS, LANES)
    occ = occupied.reshape(ROWS, LANES)
    own = [occ[: ROWS // 2], occ[ROWS // 2 :]]
    mate = [moved(v, ("orb",), lambda i: i ^ 1) for v in own]
    near = [moved(v, ("orb",), lambda i: i ^ 2) for v in own]
    far = [moved(v, ("orb",), lambda i: (i + (-4 if i & 2 else 4)) % n_orb) for v in near]
    near_mate = [moved(v, ("orb",), lambda i: i ^ 1) for v in near]
    far_mate = [moved(v, ("orb",), lambda i: i ^ 1) for v in far]

    def spread(value):
        return lax.all_to_all(value.reshape(n, part, LANES), ("grp", "orb"), split_axis=0, concat_axis=0).reshape(ROWS, LANES)

    def swapped(value):
        return moved(value, ("grp",), lambda i: i ^ 1)

    cut = target.reshape(n_orb, n_grp, part, LANES).transpose(1, 0, 2, 3)
    t_half = spread(cut)
    t_other = swapped(t_half)

    acc = pair_step(one, target, own, mate, None, False, n_grp, n_orb)
    acc = pair_step(crossed, target, near, near_mate, acc, False, n_grp, n_orb)
    acc = pair_step(one - crossed, target, far, far_mate, acc, True, n_grp, n_orb)
    x_half = spread(acc)
    x_other = swapped(x_half)

    v = potential.reshape(n_grp * part, LANES)
    gram = gram_step(x_half, t_half, lax.dynamic_slice_in_dim(v, group * part, part, 0), n, part)
    gram = summed_all(gram, n_grp, n_orb)
    return update_step(group, gram, x_half, t_half, x_other, t_other, v, n, part, n_orb)


def solution(mesh):
    placed = (P("orb", None), P(("grp", "orb"), None), P("orb"))
    return jax.shard_map(
        on_device, mesh=mesh, in_specs=placed, out_specs=P("grp", "orb"), check_vma=False
    )
```

```python
import functools

import jax
import jax.numpy as jnp
import ml_dtypes
import numpy as np
from jax import lax
from jax.experimental import pallas as pl
from jax.experimental.pallas import tpu as pltpu
from jax.sharding import PartitionSpec as P

NGRID = 64
CELLS = 262144
LANES = 128
ROWS = CELLS // LANES
SLAB = NGRID * NGRID // LANES
CHUNK = 64
LOOPS = NGRID // CHUNK

SCREEN_SQ = 0.04
BOX_LENGTH = 20.0
STEP_SIZE = 0.3

bf16 = jnp.bfloat16
f32 = jnp.float32
VMEM = pl.BlockSpec(memory_space=pltpu.VMEM)
SMEM = pl.BlockSpec(memory_space=pltpu.SMEM)


def tables():
    index = np.arange(NGRID)
    angles = 2.0 * np.pi * (index[:, None] * index[None, :] % NGRID) / NGRID
    table = np.cos(angles) + np.sin(angles)
    high = table.astype(ml_dtypes.bfloat16)
    low = (table - high.astype(np.float64)).astype(ml_dtypes.bfloat16)

    def twice(block):
        both = np.zeros((2 * NGRID, 2 * NGRID), ml_dtypes.bfloat16)
        both[:NGRID, :NGRID] = block
        both[NGRID:, NGRID:] = block
        return both

    def stacked(high, low):
        return np.concatenate([high, high, low, low], 1)

    row = np.concatenate([twice(high), twice(low)], 1)
    along_z = np.concatenate([row, row], 0)
    order = np.concatenate([index[0::2], index[1::2]])
    return (
        along_z,
        stacked(high, low),
        stacked(high[:, order], low[:, order]),
        stacked(high[order], low[order]),
    )


def halves(value):
    high = value.astype(bf16)
    return high, (value - high.astype(f32)).astype(bf16)


def dot(left, right):
    return jnp.dot(left, right, preferred_element_type=f32)


def along_lanes(value, table):
    out = dot(jnp.concatenate(halves(value), 1), table)
    return out[:, :LANES] + out[:, LANES:]


def along_rows(value, table):
    high, low = halves(value)
    return dot(table, jnp.concatenate([high, low, high, low], 0))


def beside(blocks):
    return jnp.concatenate(blocks, 1)


def apart(value):
    return [value[:, i : i + LANES] for i in range(0, value.shape[1], LANES)]


def pair_kernel(counts, has_acc, pieces, n_grp, n_orb, flags_ref, group_ref, t_ref, *refs):
    a_refs, b_refs, refs = refs[: counts[0]], refs[counts[0] : sum(counts)], refs[sum(counts) :]
    if has_acc:
        acc_ref, refs = refs[0], refs[1:]
    z_ref, x_ref, yf_ref, yi_ref, out_ref, s_ref, s2_ref = refs
    first = lax.broadcasted_iota(jnp.int32, (1, LANES), 1) < NGRID
    rows = SLAB * CHUNK
    scale_b = flags_ref[0]

    leading = group_ref[0] == 0

    def chosen(pieces):
        if len(pieces) == 1:
            return pieces[0][...]
        own, other = pieces[0][...], pieces[1][...]
        return jnp.concatenate([jnp.where(leading, own, other), jnp.where(leading, other, own)], 0)

    for c in range(LOOPS):
        t = t_ref[c * rows : (c + 1) * rows, :]
        pa = t * chosen(a_refs)
        pb = t * (chosen(b_refs) * scale_b)
        even = jnp.where(first, pa, pltpu.roll(pb, NGRID, 1)).reshape(CHUNK, SLAB, LANES)
        odd = jnp.where(first, pltpu.roll(pa, NGRID, 1), pb).reshape(CHUNK, SLAB, LANES)
        v = jnp.concatenate([even, odd], 1).reshape(CHUNK * NGRID, LANES)
        v = along_lanes(v, z_ref[...]).reshape(CHUNK, NGRID, LANES)
        v = along_rows(beside([v[i] for i in range(CHUNK)]), yf_ref[...])
        for i, block in enumerate(apart(v)):
            s_ref[(c * CHUNK + i) * NGRID : (c * CHUNK + i + 1) * NGRID, :] = block

    def squared(k):
        wave = jnp.minimum(k, NGRID - k).astype(f32) * (2.0 * np.pi / BOX_LENGTH)
        return wave * wave

    cube = (NGRID, LANES)
    base = (
        squared(lax.broadcasted_iota(jnp.int32, cube, 0))
        + squared(lax.broadcasted_iota(jnp.int32, cube, 1) % NGRID)
        + SCREEN_SQ
    )
    for c in range(LOOPS):
        v = beside([s_ref[pl.ds(c * CHUNK + i, NGRID, stride=NGRID), :] for i in range(CHUNK)])
        v = along_rows(v, x_ref[...])
        kernel = []
        for i in range(CHUNK):
            y = c * CHUNK + i
            wave = min(y, NGRID - y) * (2.0 * np.pi / BOX_LENGTH)
            kernel.append((4.0 * np.pi / CELLS) / (base + wave * wave))
        v = along_rows(v * beside(kernel), x_ref[...])
        for i, block in enumerate(apart(v)):
            s2_ref[(c * CHUNK + i) * NGRID : (c * CHUNK + i + 1) * NGRID, :] = block

    for c in range(LOOPS):
        v = beside([s2_ref[pl.ds(c * CHUNK + i, NGRID, stride=NGRID), :] for i in range(CHUNK)])
        v = jnp.concatenate(apart(along_rows(v, yi_ref[...])), 0)
        v = along_lanes(v, z_ref[...]).reshape(CHUNK, NGRID, LANES)
        even = v[:, :SLAB].reshape(rows, LANES)
        odd = v[:, SLAB:].reshape(rows, LANES)
        sa = jnp.where(first, even, pltpu.roll(odd, NGRID, 1))
        sb = jnp.where(first, pltpu.roll(even, NGRID, 1), odd)
        added = -(chosen(a_refs) * sa + (chosen(b_refs) * scale_b) * sb)
        if has_acc:
            added = acc_ref[c * rows : (c + 1) * rows, :] + added
        if pieces:
            part = ROWS // (n_grp * n_orb)
            count = n_orb // LOOPS
            cut = added.reshape(count, n_grp, part, LANES)
            for g in range(n_grp):
                start = (g * n_orb + c * count) * part
                out_ref[start : start + count * part, :] = cut[:, g].reshape(count * part, LANES)
        else:
            out_ref[c * rows : (c + 1) * rows, :] = added


def pair_step(flag, group, target, first, second, acc, cut, n_grp, n_orb):
    args = [target, *first, *second] + ([] if acc is None else [acc])
    args += [jnp.asarray(table) for table in tables()]
    return pl.pallas_call(
        functools.partial(pair_kernel, (len(first), len(second)), acc is not None, cut, n_grp, n_orb),
        out_shape=jax.ShapeDtypeStruct((ROWS, LANES), f32),
        in_specs=[SMEM] * 2 + [VMEM] * len(args),
        out_specs=VMEM,
        scratch_shapes=[pltpu.VMEM((NGRID * NGRID, LANES), f32)] * 2,
        compiler_params=pltpu.CompilerParams(vmem_limit_bytes=40 << 20),
        cost_estimate=pl.CostEstimate(flops=8 * 10**9, bytes_accessed=5 << 20, transcendentals=0),
    )(flag.reshape(1), group.reshape(1), *args)


def strided(ref, r, count, step):
    return ref[pl.ds(r, count, stride=step), :]


def gram_kernel(n, part, place_ref, x_ref, tg_ref, th_ref, v_ref, out_ref, t_ref):
    group = place_ref[0]
    x = beside([strided(x_ref, r, n, part) for r in range(part)])
    rows = th_ref.shape[0] // part
    own = beside([strided(tg_ref, group * part + r, rows, 2 * part) for r in range(part)])
    other = beside([strided(th_ref, r, rows, part) for r in range(part)])
    t = jnp.concatenate([jnp.where(group == 0, own, other), jnp.where(group == 0, other, own)], 0)
    t_ref[...] = t
    v = beside([v_ref[r : r + 1, :] for r in range(part)])
    xh, xl = halves(x)
    th, tl = halves(t)
    wh, wl = halves(t * v)
    left = jnp.concatenate([xh, th, xl, tl], 0)
    right = jnp.concatenate([xh, th, wh, xl, tl, wl], 0)
    full = lax.dot_general(left, right, (((1,), (1,)), ((), ())), preferred_element_type=f32)
    full = full[: 2 * n] + full[2 * n :]
    full = full[:, : 3 * n] + full[:, 3 * n :]
    out_ref[...] = jnp.concatenate([full[:n, : 2 * n], full[n:, 2 * n :]], 1) * (1.0 / CELLS)


def gram_step(group, x, tg, th, v, n, part):
    return pl.pallas_call(
        functools.partial(gram_kernel, n, part),
        out_shape=(
            jax.ShapeDtypeStruct((n, 3 * n), f32),
            jax.ShapeDtypeStruct((n, part * LANES), f32),
        ),
        in_specs=[SMEM] + [VMEM] * 4,
        out_specs=(VMEM, VMEM),
        compiler_params=pltpu.CompilerParams(vmem_limit_bytes=32 << 20),
        cost_estimate=pl.CostEstimate(flops=10**9, bytes_accessed=2 << 20, transcendentals=0),
    )(group.reshape(1), x, tg, th, v)


def exact(left, right, dims):
    return lax.dot_general(
        left, right, (dims, ((), ())), precision=lax.Precision.HIGHEST, preferred_element_type=f32
    )


def mixed_rows(n, part, out_rows, first, mix, x_ref, t_ref, v_ref):
    x = beside([strided(x_ref, r, n, part) for r in range(part)])
    t = t_ref[...]
    own = t_ref[pl.ds(first, out_rows), :]
    v = beside([v_ref[r : r + 1] for r in range(part)])
    xh, xl = halves(x)
    th, tl = halves(t)
    both = dot(mix, jnp.concatenate([xh, th, xl, tl], 0))
    return own * (1.0 - STEP_SIZE * v) + both[:out_rows] + both[out_rows:]


def partner_kernel(n, part, out_rows, place_ref, g_ref, x_ref, t_ref, v_ref, out_ref, mix_ref, m_ref, r_ref):
    group = place_ref[0]
    ids = lax.broadcasted_iota(jnp.int32, (n, 1), 0)
    columns = lax.broadcasted_iota(jnp.int32, (1, 3 * n), 1)
    eye = (lax.broadcasted_iota(jnp.int32, (n, n), 0) == lax.broadcasted_iota(jnp.int32, (n, n), 1)).astype(f32)
    work = jnp.concatenate([g_ref[:, : 2 * n], eye], 1)

    def eliminate(k, work):
        row = jnp.sum(jnp.where(ids == k, work, 0.0), axis=0, keepdims=True)
        pivot = jnp.sum(jnp.where(columns == k, row, 0.0), axis=1, keepdims=True)
        column = jnp.sum(jnp.where(columns == k, work, 0.0), axis=1, keepdims=True)
        root = lax.rsqrt(pivot)
        row = row * root
        lower = work - jnp.where(ids > k, column * root, 0.0) * row
        return jnp.where(ids == k, row, lower)

    work = lax.fori_loop(0, n, eliminate, work)
    pt = work[:, n : 2 * n]
    m_ref[...] = exact(pt, work[:, 2 * n :], ((0,), (0,)))
    r_ref[...] = g_ref[:, 2 * n :] - exact(pt, pt, ((0,), (0,)))

    def mixer(start):
        rows = pl.ds(start, out_rows)
        mix = jnp.concatenate([m_ref[rows, :], r_ref[rows, :]], 1) * STEP_SIZE
        high, low = halves(mix)
        return jnp.concatenate([jnp.concatenate([high, high], 1), jnp.concatenate([low, low], 1)], 0)

    mix_ref[...] = mixer(pl.multiple_of(group * out_rows, 8))
    first = pl.multiple_of((1 - group) * out_rows, 8)
    out_ref[...] = mixed_rows(n, part, out_rows, first, mixer(first), x_ref, t_ref, v_ref)


def partner_step(group, g, x, t, v, n, part, out_rows):
    return pl.pallas_call(
        functools.partial(partner_kernel, n, part, out_rows),
        out_shape=(
            jax.ShapeDtypeStruct((out_rows, part * LANES), f32),
            jax.ShapeDtypeStruct((2 * out_rows, 4 * n), bf16),
        ),
        in_specs=[SMEM] + [VMEM] * 4,
        out_specs=(VMEM, VMEM),
        scratch_shapes=[pltpu.VMEM((n, n), f32)] * 2,
        compiler_params=pltpu.CompilerParams(vmem_limit_bytes=32 << 20),
        cost_estimate=pl.CostEstimate(flops=4 * 10**9, bytes_accessed=2 << 20, transcendentals=0),
    )(group.reshape(1), g, x, t, v)


def own_kernel(n, part, out_rows, place_ref, mix_ref, x_ref, t_ref, v_ref, out_ref):
    group = place_ref[0]
    width = part * LANES
    first = pl.multiple_of(group * out_rows, 8)
    out_ref[:, pl.ds(pl.multiple_of(group * width, width), width)] = mixed_rows(
        n, part, out_rows, first, mix_ref[...], x_ref, t_ref, v_ref
    )


def own_step(group, mix, x, t, v, n, part, out_rows):
    return pl.pallas_call(
        functools.partial(own_kernel, n, part, out_rows),
        out_shape=jax.ShapeDtypeStruct((out_rows, 2 * part * LANES), f32),
        in_specs=[SMEM] + [VMEM] * 4,
        out_specs=VMEM,
        compiler_params=pltpu.CompilerParams(vmem_limit_bytes=32 << 20),
        cost_estimate=pl.CostEstimate(flops=4 * 10**9, bytes_accessed=2 << 20, transcendentals=0),
    )(group.reshape(1), mix, x, t, v)


def moved(x, axes, target):
    size = 1
    for axis in axes:
        size *= lax.axis_size(axis)
    return lax.ppermute(x, axes, [(i, target(i)) for i in range(size)])


def summed_over(x, bits):
    masks = bits if len(bits) == 1 else [bits[0], bits[1], bits[0] ^ bits[1]]
    parts = [moved(x, ("grp", "orb"), lambda i, m=m: i ^ m) for m in masks]
    for part in parts:
        x = x + part
    return x


def on_device(occupied, targets, potential):
    n_grp, n_orb = lax.axis_size("grp"), lax.axis_size("orb")
    n = n_grp * n_orb
    part = ROWS // n
    group, orb = lax.axis_index("grp"), lax.axis_index("orb")
    one = jnp.ones((), f32)
    crossed = (((orb >> 1) & 1) != (orb & 1)).astype(f32)

    def spread(value):
        return lax.all_to_all(value.reshape(n, part, LANES), ("grp", "orb"), split_axis=0, concat_axis=0).reshape(ROWS, LANES)

    def swapped(value):
        return moved(value, ("grp",), lambda i: i ^ 1)

    def mates(pieces):
        return [moved(v, ("orb",), lambda i: i ^ 1) for v in pieces]

    target = targets.reshape(ROWS, LANES)
    own = occupied.reshape(ROWS, LANES)
    mine = lax.dynamic_slice_in_dim(own, group * (ROWS // 2), ROWS // 2, 0)
    near = moved(mine, ("orb",), lambda i: i ^ 2)
    mate = mates([own])

    acc = pair_step(one, group, target, [own], mate, None, False, n_grp, n_orb)
    near, acc = lax.optimization_barrier((near, acc))
    far = moved(near, ("orb",), lambda i: (i + (-4 if i & 2 else 4)) % n_orb)
    near = [near, swapped(near)]
    far, near, target = lax.optimization_barrier((far, near, target))
    far = [far, swapped(far)]
    t_own = lax.all_to_all(target.reshape(n_orb, n_grp * part, LANES), ("orb",), split_axis=0, concat_axis=0)
    acc = pair_step(crossed, group, target, near, mates(near), acc, False, n_grp, n_orb)
    far, acc = lax.optimization_barrier((far, acc))
    acc = pair_step(one - crossed, group, target, far, mates(far), acc, True, n_grp, n_orb)
    acc, t_own = lax.optimization_barrier((acc, t_own))
    t_other = swapped(lax.dynamic_slice_in_dim(t_own, (1 - group) * part, part, 1))
    x_half = spread(acc)

    v = lax.dynamic_slice_in_dim(potential.reshape(n_grp * part, LANES), group * part, part, 0)
    gram, t_half = gram_step(
        group, x_half, t_own.reshape(ROWS, LANES), t_other.reshape(ROWS // 2, LANES), v, n, part
    )
    rest = [b for b in (1 << k for k in range(2, 30)) if b < n_orb]
    for step in [[1], [2, n_orb]] + [rest[k : k + 2] for k in range(0, len(rest), 2)]:
        gram = summed_over(gram, step)
    partner, mix = partner_step(group, gram, x_half, t_half, v, n, part, n_orb)
    update = own_step(group, mix, x_half, t_half, v, n, part, n_orb)
    width = part * LANES
    return lax.dynamic_update_slice(update, swapped(partner), (0, (1 - group) * width))


def solution(mesh):
    placed = (P("orb", None), P(("grp", "orb"), None), P("orb"))
    return jax.shard_map(
        on_device, mesh=mesh, in_specs=placed, out_specs=P("grp", "orb"), check_vma=False
    )
```

```python
import functools

import jax
import jax.numpy as jnp
import ml_dtypes
import numpy as np
from jax import lax
from jax.experimental import pallas as pl
from jax.experimental.pallas import tpu as pltpu
from jax.sharding import PartitionSpec as P

NGRID = 64
CELLS = 262144
LANES = 128
ROWS = CELLS // LANES
SLAB = NGRID * NGRID // LANES
HALF = ROWS // 2
GROUP = 32

SCREEN_SQ = 0.04
BOX_LENGTH = 20.0
STEP_SIZE = 0.3

bf16 = jnp.bfloat16
f32 = jnp.float32
VMEM = pl.BlockSpec(memory_space=pltpu.VMEM)
SMEM = pl.BlockSpec(memory_space=pltpu.SMEM)


def tables():
    index = np.arange(NGRID)
    angles = 2.0 * np.pi * (index[:, None] * index[None, :] % NGRID) / NGRID
    table = np.cos(angles) + np.sin(angles)
    high = table.astype(ml_dtypes.bfloat16)
    low = (table - high.astype(np.float64)).astype(ml_dtypes.bfloat16)

    def twice(block):
        both = np.zeros((2 * NGRID, 2 * NGRID), ml_dtypes.bfloat16)
        both[:NGRID, :NGRID] = block
        both[NGRID:, NGRID:] = block
        return both

    def stacked(high, low):
        return np.concatenate([high, high, low, np.zeros_like(low)], 1)

    row = np.concatenate([twice(high), twice(low)], 1)
    order = np.concatenate([index[0::2], index[1::2]])
    parts = [row, row, stacked(high, low), stacked(high[:, order], low[:, order])]
    return np.concatenate(parts + [stacked(high[order], low[order])], 0)


def halves(value):
    high = value.astype(bf16)
    return high, (value - high.astype(f32)).astype(bf16)


def dot(left, right):
    return jnp.dot(left, right, preferred_element_type=f32)


def along_lanes(value, table):
    out = dot(jnp.concatenate(halves(value), 1), table)
    return out[:, :LANES] + out[:, LANES:]


def along_rows(value, table):
    high, low = halves(value)
    return dot(table, jnp.concatenate([high, low, high], 0))


def beside(blocks):
    return jnp.concatenate(blocks, 1)


def apart(value):
    return [value[:, i : i + LANES] for i in range(0, value.shape[1], LANES)]


def in_order(leading, pieces):
    if len(pieces) == 1:
        return pieces[0][...]
    own, other = pieces[0][...], pieces[1][...]
    return jnp.concatenate([jnp.where(leading, own, other), jnp.where(leading, other, own)], 0)


def split_table(table_ref):
    along_z = table_ref[: 4 * NGRID, :]
    rest = [table_ref[(4 + i) * NGRID : (5 + i) * NGRID, : 3 * NGRID] for i in range(3)]
    return along_z, *rest


def first_half():
    return lax.broadcasted_iota(jnp.int32, (1, LANES), 1) < NGRID


def woven(first, a, b):
    return jnp.where(first, a, pltpu.roll(b, NGRID, 1)), jnp.where(first, pltpu.roll(a, NGRID, 1), b)


def wave(k):
    return min(k, NGRID - k) * (2.0 * np.pi / BOX_LENGTH)


def kernel_base():
    def squared(k):
        line = jnp.minimum(k, NGRID - k).astype(f32) * (2.0 * np.pi / BOX_LENGTH)
        return line * line

    cube = (NGRID, LANES)
    return (
        squared(lax.broadcasted_iota(jnp.int32, cube, 0))
        + squared(lax.broadcasted_iota(jnp.int32, cube, 1) % NGRID)
        + SCREEN_SQ
    )


def forward_zy(first, pa, pb, along_z, along_y, s_ref):
    slabs = pa.shape[0] // SLAB
    even, odd = woven(first, pa, pb)
    v = jnp.concatenate([even.reshape(slabs, SLAB, LANES), odd.reshape(slabs, SLAB, LANES)], 1)
    v = along_lanes(v.reshape(slabs * NGRID, LANES), along_z).reshape(slabs, NGRID, LANES)
    v = along_rows(beside([v[i] for i in range(slabs)]), along_y)
    for i, block in enumerate(apart(v)):
        s_ref[i * NGRID : (i + 1) * NGRID, :] = block


def backward_yz(first, start, count, step, along_y, along_z, s_ref):
    v = beside([s_ref[pl.ds(start + i, NGRID, stride=step), :] for i in range(count)])
    v = jnp.concatenate(apart(along_rows(v, along_y)), 0)
    v = along_lanes(v, along_z).reshape(count, NGRID, LANES)
    return woven(first, v[:, :SLAB].reshape(count * SLAB, LANES), v[:, SLAB:].reshape(count * SLAB, LANES))


def pair_kernel(counts, n_acc, cut, n_grp, n_orb, flag_ref, group_ref, earlier_ref, table_ref, t_ref, *refs):
    refs = list(refs)
    groups = [[refs.pop(0) for _ in range(count)] for count in counts]
    acc_refs = [refs.pop(0) for _ in range(n_acc)]
    out_ref, token_ref, s_ref, s2_ref, out_buf, out_sems = refs[:6]
    acc_bufs, acc_sems = refs[6:-1], refs[-1]
    token_ref[...] = earlier_ref[:8, :]
    loads = [
        pltpu.make_async_copy(ref, buf, acc_sems.at[i])
        for i, (ref, buf) in enumerate(zip(acc_refs, acc_bufs))
    ]
    for load in loads:
        load.start()
    first = first_half()
    leading = group_ref[0] == 0
    along_z, along_x, along_y, back_y = split_table(table_ref)

    def fields():
        b = in_order(leading, groups[1])
        if len(groups) == 3:
            b = jnp.where(flag_ref[0] > 0, b, in_order(leading, groups[2]))
        return in_order(leading, groups[0]), b

    t = t_ref[...]
    a, b = fields()
    forward_zy(first, t * a, t * b, along_z, along_y, s_ref)

    base = kernel_base()
    kernels = {}
    for y in range(NGRID // 2 + 1):
        kernels[y] = (4.0 * np.pi / CELLS) / (base + wave(y) * wave(y))
    v = beside([s_ref[pl.ds(y, NGRID, stride=NGRID), :] for y in range(NGRID)])
    v = along_rows(v, along_x) * beside([kernels[min(y, NGRID - y)] for y in range(NGRID)])
    for y, block in enumerate(apart(along_rows(v, along_x))):
        s2_ref[y * NGRID : (y + 1) * NGRID, :] = block

    for load in loads:
        load.wait()
    a, b = fields()
    stores = []
    for c in range(NGRID // GROUP):
        rows = slice(c * GROUP * SLAB, (c + 1) * GROUP * SLAB)
        sa, sb = backward_yz(first, c * GROUP, GROUP, NGRID, back_y, along_z, s2_ref)
        added = -(a[rows] * sa + b[rows] * sb)
        for buf in acc_bufs:
            added = added + buf[rows, :]
        if cut:
            part = ROWS // (n_grp * n_orb)
            count = n_orb * GROUP // NGRID
            pieces = added.reshape(count, n_grp, part, LANES)
            for g in range(n_grp):
                start = (g * n_orb + c * count) * part
                out_ref[start : start + count * part, :] = pieces[:, g].reshape(count * part, LANES)
        else:
            out_buf[rows, :] = added
            stores.append(pltpu.make_async_copy(out_buf.at[rows], out_ref.at[rows], out_sems.at[c]))
            stores[-1].start()
    for store in stores:
        store.wait()


def single_kernel(
    group_ref, earlier_ref, table_ref, t_ref, own_ref, other_ref, out_ref, token_ref, s_ref, s2_ref, out_buf, out_sems
):
    token_ref[...] = earlier_ref[:8, :]
    first = first_half()
    leading = group_ref[0] == 0
    along_z, along_x, along_y, back_y = split_table(table_ref)
    middle = NGRID // 2

    def both():
        own, other = own_ref[...], other_ref[...]
        return jnp.where(leading, own, other), jnp.where(leading, other, own)

    low, high = both()
    forward_zy(first, t_ref[:HALF, :] * low, t_ref[HALF:, :] * high, along_z, along_y, s_ref)

    base = kernel_base()
    ys = [(0, middle)] + [(y, NGRID - y) for y in range(1, middle)]
    kernel, blocks = [], []
    for y, z in ys:
        square = wave(y) * wave(y)
        if wave(y) != wave(z):
            square = jnp.where(first, square, wave(z) * wave(z))
        kernel.append((4.0 * np.pi / CELLS) / (base + square))
        top, bottom = woven(
            first, s_ref[pl.ds(y, middle, stride=NGRID), :], s_ref[pl.ds(z, middle, stride=NGRID), :]
        )
        blocks.append(jnp.concatenate([top, bottom], 0))
    v = along_rows(along_rows(beside(blocks), along_x) * beside(kernel), along_x)
    for (y, z), block in zip(ys, apart(v)):
        at_y, at_z = woven(first, block[:middle], block[middle:])
        s2_ref[y * middle : (y + 1) * middle, :] = at_y
        s2_ref[z * middle : (z + 1) * middle, :] = at_z

    low, high = both()
    sa, sb = backward_yz(first, 0, middle, middle, back_y, along_z, s2_ref)
    stores = []
    for c, value in enumerate((-(low * sa), -(high * sb))):
        rows = slice(c * HALF, (c + 1) * HALF)
        out_buf[rows, :] = value
        stores.append(pltpu.make_async_copy(out_buf.at[rows], out_ref.at[rows], out_sems.at[c]))
        stores[-1].start()
    for store in stores:
        store.wait()


ANY = pl.BlockSpec(memory_space=pl.ANY)
TOKEN = jax.ShapeDtypeStruct((8, LANES), f32)
FIELD = pltpu.HBM((ROWS, LANES), f32)


def pair_step(flag, group, token, target, fields, accs, cut, n_grp, n_orb):
    operands = [token, jnp.asarray(tables()), target] + [piece for field in fields for piece in field]
    counts = tuple(len(field) for field in fields)
    held = [pltpu.with_memory_space_constraint(acc, pltpu.HBM) for acc in accs]
    return pl.pallas_call(
        functools.partial(pair_kernel, counts, len(accs), cut, n_grp, n_orb),
        out_shape=(jax.ShapeDtypeStruct((ROWS, LANES), f32) if cut else FIELD, TOKEN),
        in_specs=[SMEM] * 2 + [VMEM] * len(operands) + [ANY] * len(accs),
        out_specs=(VMEM if cut else ANY, VMEM),
        scratch_shapes=[pltpu.VMEM((NGRID * NGRID, LANES), f32)] * 2
        + [pltpu.VMEM((ROWS, LANES), f32), pltpu.SemaphoreType.DMA((2,))]
        + [pltpu.VMEM((ROWS, LANES), f32)] * len(accs)
        + [pltpu.SemaphoreType.DMA((max(len(accs), 1),))],
        compiler_params=pltpu.CompilerParams(vmem_limit_bytes=44 << 20),
        cost_estimate=pl.CostEstimate(flops=10**8 if cut else 8 * 10**9, bytes_accessed=1 << 18, transcendentals=0),
    )(flag.reshape(1), group.reshape(1), *operands, *held)


def single_step(group, token, target, pieces):
    return pl.pallas_call(
        single_kernel,
        out_shape=(FIELD, TOKEN),
        in_specs=[SMEM] + [VMEM] * 5,
        out_specs=(ANY, VMEM),
        scratch_shapes=[pltpu.VMEM((NGRID * NGRID // 2, LANES), f32)] * 2
        + [pltpu.VMEM((ROWS, LANES), f32), pltpu.SemaphoreType.DMA((2,))],
        compiler_params=pltpu.CompilerParams(vmem_limit_bytes=40 << 20),
        cost_estimate=pl.CostEstimate(flops=10**10, bytes_accessed=4 << 20, transcendentals=0),
    )(group.reshape(1), token, jnp.asarray(tables()), target, *pieces)


def strided(ref, r, count, step):
    return ref[pl.ds(r, count, stride=step), :]


def gram_kernel(n, part, place_ref, x_ref, tl_ref, tu_ref, th_ref, v_ref, out_ref, t_ref):
    group = place_ref[0]
    x = beside([strided(x_ref, r, n, part) for r in range(part)])
    rows = th_ref.shape[0] // part
    low = beside([strided(tl_ref, r, rows, part) for r in range(part)])
    high = beside([strided(tu_ref, r, rows, part) for r in range(part)])
    own = jnp.where(group == 0, low, high)
    other = beside([strided(th_ref, r, rows, part) for r in range(part)])
    t = jnp.concatenate([jnp.where(group == 0, own, other), jnp.where(group == 0, other, own)], 0)
    t_ref[...] = t
    v = beside([v_ref[r : r + 1, :] for r in range(part)])
    xh, xl = halves(x)
    th, tl = halves(t)
    wh, wl = halves(t * v)
    left = jnp.concatenate([xh, th, xl, tl], 0)
    right = jnp.concatenate([xh, th, wh, xl, tl, wl], 0)
    full = lax.dot_general(left, right, (((1,), (1,)), ((), ())), preferred_element_type=f32)
    full = full[: 2 * n] + full[2 * n :]
    full = full[:, : 3 * n] + full[:, 3 * n :]
    out_ref[...] = jnp.concatenate([full[:n, : 2 * n], full[n:, 2 * n :]], 1) * (1.0 / CELLS)


def gram_step(group, x, tl, tu, th, v, n, part):
    return pl.pallas_call(
        functools.partial(gram_kernel, n, part),
        out_shape=(
            jax.ShapeDtypeStruct((n, 3 * n), f32),
            jax.ShapeDtypeStruct((n, part * LANES), f32),
        ),
        in_specs=[SMEM] + [VMEM] * 5,
        out_specs=(VMEM, VMEM),
        compiler_params=pltpu.CompilerParams(vmem_limit_bytes=32 << 20),
        cost_estimate=pl.CostEstimate(flops=10**9, bytes_accessed=2 << 20, transcendentals=0),
    )(group.reshape(1), x, tl, tu, th, v)


def exact(left, right, dims):
    return lax.dot_general(
        left, right, (dims, ((), ())), precision=lax.Precision.HIGHEST, preferred_element_type=f32
    )


def mixed_rows(n, part, out_rows, first, mix, x_ref, t_ref, v_ref):
    x = beside([strided(x_ref, r, n, part) for r in range(part)])
    t = t_ref[...]
    own = t_ref[pl.ds(first, out_rows), :]
    v = beside([v_ref[r : r + 1] for r in range(part)])
    xh, xl = halves(x)
    th, tl = halves(t)
    both = dot(mix, jnp.concatenate([xh, th, xl, tl], 0))
    return own * (1.0 - STEP_SIZE * v) + both[:out_rows] + both[out_rows:]


def eliminated(work, n):
    ids = lax.broadcasted_iota(jnp.int32, (8, 1), 0)
    blocks = [work[i : i + 8] for i in range(0, n, 8)]
    for k in range(n):
        at, inside = divmod(k, 8)
        row = blocks[at][inside : inside + 1]
        root = lax.rsqrt(row[:, k : k + 1])
        row = row * root
        for i in range(at, len(blocks)):
            column = blocks[i][:, k : k + 1] * root
            if i > at:
                blocks[i] = blocks[i] - column * row
            else:
                lower = blocks[i] - jnp.where(ids > inside, column, 0.0) * row
                blocks[i] = jnp.where(ids == inside, row, lower)
    return jnp.concatenate(blocks, 0)


def partner_kernel(n, part, out_rows, place_ref, g_ref, x_ref, t_ref, v_ref, out_ref, mix_ref, m_ref, r_ref):
    group = place_ref[0]
    ids = lax.broadcasted_iota(jnp.int32, (n, 1), 0)
    columns = lax.broadcasted_iota(jnp.int32, (1, 3 * n), 1)
    eye = (lax.broadcasted_iota(jnp.int32, (n, n), 0) == lax.broadcasted_iota(jnp.int32, (n, n), 1)).astype(f32)
    work = jnp.concatenate([g_ref[:, : 2 * n], eye], 1)

    def eliminate(k, work):
        row = jnp.sum(jnp.where(ids == k, work, 0.0), axis=0, keepdims=True)
        pivot = jnp.sum(jnp.where(columns == k, row, 0.0), axis=1, keepdims=True)
        column = jnp.sum(jnp.where(columns == k, work, 0.0), axis=1, keepdims=True)
        root = lax.rsqrt(pivot)
        row = row * root
        lower = work - jnp.where(ids > k, column * root, 0.0) * row
        return jnp.where(ids == k, row, lower)

    work = eliminated(work, n) if n <= 32 else lax.fori_loop(0, n, eliminate, work)
    pt = work[:, n : 2 * n]
    m_ref[...] = exact(pt, work[:, 2 * n :], ((0,), (0,)))
    r_ref[...] = g_ref[:, 2 * n :] - exact(pt, pt, ((0,), (0,)))

    def mixer(start):
        rows = pl.ds(start, out_rows)
        mix = jnp.concatenate([m_ref[rows, :], r_ref[rows, :]], 1) * STEP_SIZE
        high, low = halves(mix)
        return jnp.concatenate([jnp.concatenate([high, high], 1), jnp.concatenate([low, low], 1)], 0)

    mix_ref[...] = mixer(pl.multiple_of(group * out_rows, 8))
    first = pl.multiple_of((1 - group) * out_rows, 8)
    out_ref[...] = mixed_rows(n, part, out_rows, first, mixer(first), x_ref, t_ref, v_ref)


def partner_step(group, g, x, t, v, n, part, out_rows):
    return pl.pallas_call(
        functools.partial(partner_kernel, n, part, out_rows),
        out_shape=(
            jax.ShapeDtypeStruct((out_rows, part * LANES), f32),
            jax.ShapeDtypeStruct((2 * out_rows, 4 * n), bf16),
        ),
        in_specs=[SMEM] + [VMEM] * 4,
        out_specs=(VMEM, VMEM),
        scratch_shapes=[pltpu.VMEM((n, n), f32)] * 2,
        compiler_params=pltpu.CompilerParams(vmem_limit_bytes=32 << 20),
        cost_estimate=pl.CostEstimate(flops=4 * 10**9, bytes_accessed=2 << 20, transcendentals=0),
    )(group.reshape(1), g, x, t, v)


def own_kernel(n, part, out_rows, place_ref, mix_ref, x_ref, t_ref, v_ref, out_ref):
    group = place_ref[0]
    width = part * LANES
    first = pl.multiple_of(group * out_rows, 8)
    out_ref[:, pl.ds(pl.multiple_of(group * width, width), width)] = mixed_rows(
        n, part, out_rows, first, mix_ref[...], x_ref, t_ref, v_ref
    )


def own_step(group, mix, x, t, v, n, part, out_rows):
    return pl.pallas_call(
        functools.partial(own_kernel, n, part, out_rows),
        out_shape=jax.ShapeDtypeStruct((out_rows, 2 * part * LANES), f32),
        in_specs=[SMEM] + [VMEM] * 4,
        out_specs=VMEM,
        compiler_params=pltpu.CompilerParams(vmem_limit_bytes=32 << 20),
        cost_estimate=pl.CostEstimate(flops=4 * 10**9, bytes_accessed=2 << 20, transcendentals=0),
    )(group.reshape(1), mix, x, t, v)


def moved(x, axes, target):
    size = 1
    for axis in axes:
        size *= lax.axis_size(axis)
    return lax.ppermute(x, axes, [(i, target(i)) for i in range(size)])


def summed_over(x, bits):
    masks = bits if len(bits) == 1 else [bits[0], bits[1], bits[0] ^ bits[1]]
    parts = [moved(x, ("grp", "orb"), lambda i, m=m: i ^ m) for m in masks]
    for part in parts:
        x = x + part
    return x


def on_device(occupied, targets, potential):
    n_grp, n_orb = lax.axis_size("grp"), lax.axis_size("orb")
    n = n_grp * n_orb
    part = ROWS // n
    group, orb = lax.axis_index("grp"), lax.axis_index("orb")
    one = jnp.ones((), f32)
    crossed = (((orb >> 1) & 1) != (orb & 1)).astype(f32)

    def spread(value):
        return lax.all_to_all(value.reshape(n, part, LANES), ("grp", "orb"), split_axis=0, concat_axis=0).reshape(ROWS, LANES)

    def swapped(value):
        return moved(value, ("grp",), lambda i: i ^ 1)

    def mates(pieces):
        return [moved(v, ("orb",), lambda i: i ^ 1) for v in pieces]

    target = targets.reshape(ROWS, LANES)
    own = occupied.reshape(ROWS, LANES)
    mine = lax.dynamic_slice_in_dim(own, group * (ROWS // 2), ROWS // 2, 0)
    near = moved(mine, ("orb",), lambda i: i ^ 2)
    mate = mates([own])

    def owned(value, start):
        piece = value.reshape(n_orb, n_grp * part, LANES)[:, start : start + part]
        return lax.all_to_all(piece, ("orb",), split_axis=0, concat_axis=0).reshape(HALF, LANES)

    t_low = owned(target, 0)
    near, token = lax.optimization_barrier((near, potential.reshape(-1, LANES)))
    begun, token = pair_step(one, group, token, target, [[own], mate], [], False, n_grp, n_orb)
    far = moved(near, ("orb",), lambda i: (i + (-4 if i & 2 else 4)) % n_orb)
    near = [near, swapped(near)]
    far, near, late, token, t_low = lax.optimization_barrier((far, near, target, token, t_low))
    far = [far, swapped(far)]
    near_mate = mates(near)
    t_high = owned(late, part)
    going, token = single_step(group, token, target, near)
    far, token = lax.optimization_barrier((far, token))
    fields = [far, near_mate, mates(far)]
    acc, token = pair_step(crossed, group, token, target, fields, [begun, going], True, n_grp, n_orb)
    acc, t_low, t_high = lax.optimization_barrier((acc, t_low, t_high))
    t_other = swapped(jnp.where(group == 0, t_high, t_low))
    x_half = spread(acc)

    v = lax.dynamic_slice_in_dim(potential.reshape(n_grp * part, LANES), group * part, part, 0)
    gram, t_half = gram_step(group, x_half, t_low, t_high, t_other, v, n, part)
    rest = [b for b in (1 << k for k in range(2, 30)) if b < n_orb]
    for step in [[1], [2, n_orb]] + [rest[k : k + 2] for k in range(0, len(rest), 2)]:
        gram = summed_over(gram, step)
    partner, mix = partner_step(group, gram, x_half, t_half, v, n, part, n_orb)
    update = own_step(group, mix, x_half, t_half, v, n, part, n_orb)
    width = part * LANES
    return lax.dynamic_update_slice(update, swapped(partner), (0, (1 - group) * width))


def solution(mesh):
    placed = (P("orb", None), P(("grp", "orb"), None), P("orb"))
    return jax.shard_map(
        on_device, mesh=mesh, in_specs=placed, out_specs=P("grp", "orb"), check_vma=False
    )
```

```python
import functools

import jax
import jax.numpy as jnp
import ml_dtypes
import numpy as np
from jax import lax
from jax.experimental import pallas as pl
from jax.experimental.pallas import tpu as pltpu
from jax.sharding import PartitionSpec as P

NGRID = 64
CELLS = 262144
LANES = 128
ROWS = CELLS // LANES
SLAB = NGRID * NGRID // LANES
HALF = ROWS // 2
GROUP = 32

SCREEN_SQ = 0.04
BOX_LENGTH = 20.0
STEP_SIZE = 0.3

bf16 = jnp.bfloat16
f32 = jnp.float32
VMEM = pl.BlockSpec(memory_space=pltpu.VMEM)
SMEM = pl.BlockSpec(memory_space=pltpu.SMEM)


def tables():
    index = np.arange(NGRID)
    angles = 2.0 * np.pi * (index[:, None] * index[None, :] % NGRID) / NGRID
    table = np.cos(angles) + np.sin(angles)
    high = table.astype(ml_dtypes.bfloat16)
    low = (table - high.astype(np.float64)).astype(ml_dtypes.bfloat16)

    def twice(block):
        both = np.zeros((2 * NGRID, 2 * NGRID), ml_dtypes.bfloat16)
        both[:NGRID, :NGRID] = block
        both[NGRID:, NGRID:] = block
        return both

    def stacked(high, low):
        return np.concatenate([high, high, low, np.zeros_like(low)], 1)

    row = np.concatenate([twice(high), twice(low)], 1)
    order = np.concatenate([index[0::2], index[1::2]])
    parts = [row, row, stacked(high, low), stacked(high[:, order], low[:, order])]
    return np.concatenate(parts + [stacked(high[order], low[order])], 0)


def halves(value):
    high = value.astype(bf16)
    return high, (value - high.astype(f32)).astype(bf16)


def dot(left, right):
    return jnp.dot(left, right, preferred_element_type=f32)


def along_lanes(value, table):
    out = dot(jnp.concatenate(halves(value), 1), table)
    return out[:, :LANES] + out[:, LANES:]


def along_rows(value, table):
    high, low = halves(value)
    return dot(table, jnp.concatenate([high, low, high], 0))


def beside(blocks):
    return jnp.concatenate(blocks, 1)


def apart(value):
    return [value[:, i : i + LANES] for i in range(0, value.shape[1], LANES)]


def in_order(leading, pieces):
    if len(pieces) == 1:
        return pieces[0][...]
    own, other = pieces[0][...], pieces[1][...]
    return jnp.concatenate([jnp.where(leading, own, other), jnp.where(leading, other, own)], 0)


def split_table(table_ref):
    along_z = table_ref[: 4 * NGRID, :]
    rest = [table_ref[(4 + i) * NGRID : (5 + i) * NGRID, : 3 * NGRID] for i in range(3)]
    return along_z, *rest


def first_half():
    return lax.broadcasted_iota(jnp.int32, (1, LANES), 1) < NGRID


def woven(first, a, b):
    return jnp.where(first, a, pltpu.roll(b, NGRID, 1)), jnp.where(first, pltpu.roll(a, NGRID, 1), b)


def wave(k):
    return min(k, NGRID - k) * (2.0 * np.pi / BOX_LENGTH)


def kernel_base():
    def squared(k):
        line = jnp.minimum(k, NGRID - k).astype(f32) * (2.0 * np.pi / BOX_LENGTH)
        return line * line

    cube = (NGRID, LANES)
    return (
        squared(lax.broadcasted_iota(jnp.int32, cube, 0))
        + squared(lax.broadcasted_iota(jnp.int32, cube, 1) % NGRID)
        + SCREEN_SQ
    )


def forward_zy(first, pa, pb, along_z, along_y, s_ref):
    slabs = pa.shape[0] // SLAB
    even, odd = woven(first, pa, pb)
    v = jnp.concatenate([even.reshape(slabs, SLAB, LANES), odd.reshape(slabs, SLAB, LANES)], 1)
    v = along_lanes(v.reshape(slabs * NGRID, LANES), along_z).reshape(slabs, NGRID, LANES)
    v = along_rows(beside([v[i] for i in range(slabs)]), along_y)
    for i, block in enumerate(apart(v)):
        s_ref[i * NGRID : (i + 1) * NGRID, :] = block


def backward_yz(first, start, count, step, along_y, along_z, s_ref):
    v = beside([s_ref[pl.ds(start + i, NGRID, stride=step), :] for i in range(count)])
    v = jnp.concatenate(apart(along_rows(v, along_y)), 0)
    v = along_lanes(v, along_z).reshape(count, NGRID, LANES)
    return woven(first, v[:, :SLAB].reshape(count * SLAB, LANES), v[:, SLAB:].reshape(count * SLAB, LANES))


def pair_kernel(counts, n_acc, cut, n_grp, n_orb, flag_ref, group_ref, earlier_ref, table_ref, t_ref, *refs):
    refs = list(refs)
    groups = [[refs.pop(0) for _ in range(count)] for count in counts]
    acc_refs = [refs.pop(0) for _ in range(n_acc)]
    out_ref, token_ref, s_ref, s2_ref, kept_ref, out_buf, out_sems = refs[:7]
    acc_bufs, acc_sems = refs[7:-1], refs[-1]
    token_ref[...] = earlier_ref[:8, :]
    loads = [
        pltpu.make_async_copy(ref, buf, acc_sems.at[i])
        for i, (ref, buf) in enumerate(zip(acc_refs, acc_bufs))
    ]
    for load in loads:
        load.start()
    first = first_half()
    leading = group_ref[0] == 0
    along_z, along_x, along_y, back_y = split_table(table_ref)

    def fields():
        b = in_order(leading, groups[1])
        if len(groups) == 3:
            b = jnp.where(flag_ref[0] > 0, b, in_order(leading, groups[2]))
        return in_order(leading, groups[0]), b

    t = t_ref[...]
    a, b = fields()
    kept_ref[0], kept_ref[1] = a, b
    forward_zy(first, t * a, t * b, along_z, along_y, s_ref)

    base = kernel_base()
    kernels = {}
    for y in range(NGRID // 2 + 1):
        kernels[y] = (4.0 * np.pi / CELLS) / (base + wave(y) * wave(y))
    v = beside([s_ref[pl.ds(y, NGRID, stride=NGRID), :] for y in range(NGRID)])
    v = along_rows(v, along_x) * beside([kernels[min(y, NGRID - y)] for y in range(NGRID)])
    for y, block in enumerate(apart(along_rows(v, along_x))):
        s2_ref[y * NGRID : (y + 1) * NGRID, :] = block

    for load in loads:
        load.wait()
    stores = []
    for c in range(NGRID // GROUP):
        rows = slice(c * GROUP * SLAB, (c + 1) * GROUP * SLAB)
        sa, sb = backward_yz(first, c * GROUP, GROUP, NGRID, back_y, along_z, s2_ref)
        added = -(kept_ref[0, rows, :] * sa + kept_ref[1, rows, :] * sb)
        for buf in acc_bufs:
            added = added + buf[rows, :]
        if cut:
            part = ROWS // (n_grp * n_orb)
            count = n_orb * GROUP // NGRID
            pieces = added.reshape(count, n_grp, part, LANES)
            for g in range(n_grp):
                start = (g * n_orb + c * count) * part
                out_ref[start : start + count * part, :] = pieces[:, g].reshape(count * part, LANES)
        else:
            out_buf[rows, :] = added
            stores.append(pltpu.make_async_copy(out_buf.at[rows], out_ref.at[rows], out_sems.at[c]))
            stores[-1].start()
    for store in stores:
        store.wait()


def single_kernel(
    group_ref, earlier_ref, table_ref, t_ref, own_ref, other_ref, out_ref, token_ref, s_ref, s2_ref, out_buf, out_sems
):
    token_ref[...] = earlier_ref[:8, :]
    first = first_half()
    leading = group_ref[0] == 0
    along_z, along_x, along_y, back_y = split_table(table_ref)
    middle = NGRID // 2

    def both():
        own, other = own_ref[...], other_ref[...]
        return jnp.where(leading, own, other), jnp.where(leading, other, own)

    low, high = both()
    forward_zy(first, t_ref[:HALF, :] * low, t_ref[HALF:, :] * high, along_z, along_y, s_ref)

    base = kernel_base()
    ys = [(0, middle)] + [(y, NGRID - y) for y in range(1, middle)]
    kernel, blocks = [], []
    for y, z in ys:
        square = wave(y) * wave(y)
        if wave(y) != wave(z):
            square = jnp.where(first, square, wave(z) * wave(z))
        kernel.append((4.0 * np.pi / CELLS) / (base + square))
        top, bottom = woven(
            first, s_ref[pl.ds(y, middle, stride=NGRID), :], s_ref[pl.ds(z, middle, stride=NGRID), :]
        )
        blocks.append(jnp.concatenate([top, bottom], 0))
    v = along_rows(along_rows(beside(blocks), along_x) * beside(kernel), along_x)
    for (y, z), block in zip(ys, apart(v)):
        at_y, at_z = woven(first, block[:middle], block[middle:])
        s2_ref[y * middle : (y + 1) * middle, :] = at_y
        s2_ref[z * middle : (z + 1) * middle, :] = at_z

    low, high = both()
    sa, sb = backward_yz(first, 0, middle, middle, back_y, along_z, s2_ref)
    stores = []
    for c, value in enumerate((-(low * sa), -(high * sb))):
        rows = slice(c * HALF, (c + 1) * HALF)
        out_buf[rows, :] = value
        stores.append(pltpu.make_async_copy(out_buf.at[rows], out_ref.at[rows], out_sems.at[c]))
        stores[-1].start()
    for store in stores:
        store.wait()


ANY = pl.BlockSpec(memory_space=pl.ANY)
TOKEN = jax.ShapeDtypeStruct((8, LANES), f32)
FIELD = pltpu.HBM((ROWS, LANES), f32)


def pair_step(flag, group, token, target, fields, accs, cut, n_grp, n_orb):
    operands = [token, jnp.asarray(tables()), target] + [piece for field in fields for piece in field]
    counts = tuple(len(field) for field in fields)
    held = [pltpu.with_memory_space_constraint(acc, pltpu.HBM) for acc in accs]
    return pl.pallas_call(
        functools.partial(pair_kernel, counts, len(accs), cut, n_grp, n_orb),
        out_shape=(jax.ShapeDtypeStruct((ROWS, LANES), f32) if cut else FIELD, TOKEN),
        in_specs=[SMEM] * 2 + [VMEM] * len(operands) + [ANY] * len(accs),
        out_specs=(VMEM if cut else ANY, VMEM),
        scratch_shapes=[pltpu.VMEM((NGRID * NGRID, LANES), f32)] * 2
        + [pltpu.VMEM((2, ROWS, LANES), f32)]
        + [pltpu.VMEM((ROWS, LANES), f32), pltpu.SemaphoreType.DMA((2,))]
        + [pltpu.VMEM((ROWS, LANES), f32)] * len(accs)
        + [pltpu.SemaphoreType.DMA((max(len(accs), 1),))],
        compiler_params=pltpu.CompilerParams(vmem_limit_bytes=44 << 20),
        cost_estimate=pl.CostEstimate(flops=10**8 if cut else 8 * 10**9, bytes_accessed=1 << 18, transcendentals=0),
    )(flag.reshape(1), group.reshape(1), *operands, *held)


def single_step(group, token, target, pieces):
    return pl.pallas_call(
        single_kernel,
        out_shape=(FIELD, TOKEN),
        in_specs=[SMEM] + [VMEM] * 5,
        out_specs=(ANY, VMEM),
        scratch_shapes=[pltpu.VMEM((NGRID * NGRID // 2, LANES), f32)] * 2
        + [pltpu.VMEM((ROWS, LANES), f32), pltpu.SemaphoreType.DMA((2,))],
        compiler_params=pltpu.CompilerParams(vmem_limit_bytes=40 << 20),
        cost_estimate=pl.CostEstimate(flops=10**10, bytes_accessed=4 << 20, transcendentals=0),
    )(group.reshape(1), token, jnp.asarray(tables()), target, *pieces)


def strided(ref, r, count, step):
    return ref[pl.ds(r, count, stride=step), :]


def gram_kernel(n, part, place_ref, x_ref, tl_ref, tu_ref, th_ref, v_ref, out_ref, t_ref):
    group = place_ref[0]
    x = beside([strided(x_ref, r, n, part) for r in range(part)])
    rows = th_ref.shape[0] // part
    low = beside([strided(tl_ref, r, rows, part) for r in range(part)])
    high = beside([strided(tu_ref, r, rows, part) for r in range(part)])
    own = jnp.where(group == 0, low, high)
    other = beside([strided(th_ref, r, rows, part) for r in range(part)])
    t = jnp.concatenate([jnp.where(group == 0, own, other), jnp.where(group == 0, other, own)], 0)
    t_ref[...] = t
    v = beside([v_ref[r : r + 1, :] for r in range(part)])
    xh, xl = halves(x)
    th, tl = halves(t)
    wh, wl = halves(t * v)
    left = jnp.concatenate([xh, th, xl, tl], 0)
    right = jnp.concatenate([xh, th, wh, xl, tl, wl], 0)
    full = lax.dot_general(left, right, (((1,), (1,)), ((), ())), preferred_element_type=f32)
    full = full[: 2 * n] + full[2 * n :]
    full = full[:, : 3 * n] + full[:, 3 * n :]
    out_ref[...] = jnp.concatenate([full[:n, : 2 * n], full[n:, 2 * n :]], 1) * (1.0 / CELLS)


def gram_step(group, x, tl, tu, th, v, n, part):
    return pl.pallas_call(
        functools.partial(gram_kernel, n, part),
        out_shape=(
            jax.ShapeDtypeStruct((n, 3 * n), f32),
            jax.ShapeDtypeStruct((n, part * LANES), f32),
        ),
        in_specs=[SMEM] + [VMEM] * 5,
        out_specs=(VMEM, VMEM),
        compiler_params=pltpu.CompilerParams(vmem_limit_bytes=32 << 20),
        cost_estimate=pl.CostEstimate(flops=10**9, bytes_accessed=2 << 20, transcendentals=0),
    )(group.reshape(1), x, tl, tu, th, v)


def exact(left, right, dims):
    return lax.dot_general(
        left, right, (dims, ((), ())), precision=lax.Precision.HIGHEST, preferred_element_type=f32
    )


def mixed_rows(n, part, out_rows, first, mix, x_ref, t_ref, v_ref):
    x = beside([strided(x_ref, r, n, part) for r in range(part)])
    t = t_ref[...]
    own = t_ref[pl.ds(first, out_rows), :]
    v = beside([v_ref[r : r + 1] for r in range(part)])
    xh, xl = halves(x)
    th, tl = halves(t)
    both = dot(mix, jnp.concatenate([xh, th, xl, tl], 0))
    return own * (1.0 - STEP_SIZE * v) + both[:out_rows] + both[out_rows:]


def eliminated(work, n):
    ids = lax.broadcasted_iota(jnp.int32, (8, 1), 0)
    blocks = [work[i : i + 8] for i in range(0, n, 8)]
    for k in range(n):
        at, inside = divmod(k, 8)
        row = blocks[at][inside : inside + 1]
        root = lax.rsqrt(row[:, k : k + 1])
        row = row * root
        for i in range(at, len(blocks)):
            column = blocks[i][:, k : k + 1] * root
            if i > at:
                blocks[i] = blocks[i] - column * row
            else:
                lower = blocks[i] - jnp.where(ids > inside, column, 0.0) * row
                blocks[i] = jnp.where(ids == inside, row, lower)
    return jnp.concatenate(blocks, 0)


def partner_kernel(n, part, out_rows, place_ref, g_ref, x_ref, t_ref, v_ref, out_ref, mix_ref, m_ref, r_ref):
    group = place_ref[0]
    ids = lax.broadcasted_iota(jnp.int32, (n, 1), 0)
    columns = lax.broadcasted_iota(jnp.int32, (1, 3 * n), 1)
    eye = (lax.broadcasted_iota(jnp.int32, (n, n), 0) == lax.broadcasted_iota(jnp.int32, (n, n), 1)).astype(f32)
    work = jnp.concatenate([g_ref[:, : 2 * n], eye], 1)

    def eliminate(k, work):
        row = jnp.sum(jnp.where(ids == k, work, 0.0), axis=0, keepdims=True)
        pivot = jnp.sum(jnp.where(columns == k, row, 0.0), axis=1, keepdims=True)
        column = jnp.sum(jnp.where(columns == k, work, 0.0), axis=1, keepdims=True)
        root = lax.rsqrt(pivot)
        row = row * root
        lower = work - jnp.where(ids > k, column * root, 0.0) * row
        return jnp.where(ids == k, row, lower)

    work = eliminated(work, n) if n <= 32 else lax.fori_loop(0, n, eliminate, work)
    pt = work[:, n : 2 * n]
    m_ref[...] = exact(pt, work[:, 2 * n :], ((0,), (0,)))
    r_ref[...] = g_ref[:, 2 * n :] - exact(pt, pt, ((0,), (0,)))

    def mixer(start):
        rows = pl.ds(start, out_rows)
        mix = jnp.concatenate([m_ref[rows, :], r_ref[rows, :]], 1) * STEP_SIZE
        high, low = halves(mix)
        return jnp.concatenate([jnp.concatenate([high, high], 1), jnp.concatenate([low, low], 1)], 0)

    mix_ref[...] = mixer(pl.multiple_of(group * out_rows, 8))
    first = pl.multiple_of((1 - group) * out_rows, 8)
    out_ref[...] = mixed_rows(n, part, out_rows, first, mixer(first), x_ref, t_ref, v_ref)


def partner_step(group, g, x, t, v, n, part, out_rows):
    return pl.pallas_call(
        functools.partial(partner_kernel, n, part, out_rows),
        out_shape=(
            jax.ShapeDtypeStruct((out_rows, part * LANES), f32),
            jax.ShapeDtypeStruct((2 * out_rows, 4 * n), bf16),
        ),
        in_specs=[SMEM] + [VMEM] * 4,
        out_specs=(VMEM, VMEM),
        scratch_shapes=[pltpu.VMEM((n, n), f32)] * 2,
        compiler_params=pltpu.CompilerParams(vmem_limit_bytes=32 << 20),
        cost_estimate=pl.CostEstimate(flops=4 * 10**9, bytes_accessed=2 << 20, transcendentals=0),
    )(group.reshape(1), g, x, t, v)


def own_kernel(n, part, out_rows, place_ref, mix_ref, x_ref, t_ref, v_ref, out_ref):
    group = place_ref[0]
    width = part * LANES
    first = pl.multiple_of(group * out_rows, 8)
    out_ref[:, pl.ds(pl.multiple_of(group * width, width), width)] = mixed_rows(
        n, part, out_rows, first, mix_ref[...], x_ref, t_ref, v_ref
    )


def own_step(group, mix, x, t, v, n, part, out_rows):
    return pl.pallas_call(
        functools.partial(own_kernel, n, part, out_rows),
        out_shape=jax.ShapeDtypeStruct((out_rows, 2 * part * LANES), f32),
        in_specs=[SMEM] + [VMEM] * 4,
        out_specs=VMEM,
        compiler_params=pltpu.CompilerParams(vmem_limit_bytes=32 << 20),
        cost_estimate=pl.CostEstimate(flops=4 * 10**9, bytes_accessed=2 << 20, transcendentals=0),
    )(group.reshape(1), mix, x, t, v)


def moved(x, axes, target):
    size = 1
    for axis in axes:
        size *= lax.axis_size(axis)
    return lax.ppermute(x, axes, [(i, target(i)) for i in range(size)])


def summed_over(x, bits):
    masks = bits if len(bits) == 1 else [bits[0], bits[1], bits[0] ^ bits[1]]
    parts = [moved(x, ("grp", "orb"), lambda i, m=m: i ^ m) for m in masks]
    for part in parts:
        x = x + part
    return x


def on_device(occupied, targets, potential):
    n_grp, n_orb = lax.axis_size("grp"), lax.axis_size("orb")
    n = n_grp * n_orb
    part = ROWS // n
    group, orb = lax.axis_index("grp"), lax.axis_index("orb")
    one = jnp.ones((), f32)
    crossed = (((orb >> 1) & 1) != (orb & 1)).astype(f32)

    def spread(value):
        return lax.all_to_all(value.reshape(n, part, LANES), ("grp", "orb"), split_axis=0, concat_axis=0).reshape(ROWS, LANES)

    def swapped(value):
        return moved(value, ("grp",), lambda i: i ^ 1)

    def mates(pieces):
        return [moved(v, ("orb",), lambda i: i ^ 1) for v in pieces]

    target = targets.reshape(ROWS, LANES)
    own = occupied.reshape(ROWS, LANES)
    mine = lax.dynamic_slice_in_dim(own, group * (ROWS // 2), ROWS // 2, 0)
    near = moved(mine, ("orb",), lambda i: i ^ 2)
    mate = mates([own])

    def owned(value, start):
        piece = value.reshape(n_orb, n_grp * part, LANES)[:, start : start + part]
        return lax.all_to_all(piece, ("orb",), split_axis=0, concat_axis=0).reshape(HALF, LANES)

    t_low = owned(target, 0)
    near, token = lax.optimization_barrier((near, potential.reshape(-1, LANES)))
    begun, token = pair_step(one, group, token, target, [[own], mate], [], False, n_grp, n_orb)
    far = moved(near, ("orb",), lambda i: (i + (-4 if i & 2 else 4)) % n_orb)
    near = [near, swapped(near)]
    far, near, late, token, t_low = lax.optimization_barrier((far, near, target, token, t_low))
    far = [far, swapped(far)]
    near_mate = mates(near)
    t_high = owned(late, part)
    going, token = single_step(group, token, target, near)
    far, token = lax.optimization_barrier((far, token))
    fields = [far, near_mate, mates(far)]
    acc, token = pair_step(crossed, group, token, target, fields, [begun, going], True, n_grp, n_orb)
    acc, t_low, t_high = lax.optimization_barrier((acc, t_low, t_high))
    t_other = swapped(jnp.where(group == 0, t_high, t_low))
    x_half = spread(acc)

    v = lax.dynamic_slice_in_dim(potential.reshape(n_grp * part, LANES), group * part, part, 0)
    gram, t_half = gram_step(group, x_half, t_low, t_high, t_other, v, n, part)
    rest = [b for b in (1 << k for k in range(2, 30)) if b < n_orb]
    for step in [[1]] + [rest[k : k + 2] for k in range(0, len(rest), 2)] + [[2, n_orb]]:
        gram = summed_over(gram, step)
    partner, mix = partner_step(group, gram, x_half, t_half, v, n, part, n_orb)
    update = own_step(group, mix, x_half, t_half, v, n, part, n_orb)
    width = part * LANES
    return lax.dynamic_update_slice(update, swapped(partner), (0, (1 - group) * width))


def solution(mesh):
    placed = (P("orb", None), P(("grp", "orb"), None), P("orb"))
    return jax.shard_map(
        on_device, mesh=mesh, in_specs=placed, out_specs=P("grp", "orb"), check_vma=False
    )
```

```python
import functools

import jax
import jax.numpy as jnp
import ml_dtypes
import numpy as np
from jax import lax
from jax.experimental import pallas as pl
from jax.experimental.pallas import tpu as pltpu
from jax.sharding import PartitionSpec as P

NGRID = 64
CELLS = 262144
LANES = 128
ROWS = CELLS // LANES
SLAB = NGRID * NGRID // LANES
HALF = ROWS // 2
GROUP = 32

SCREEN_SQ = 0.04
BOX_LENGTH = 20.0
STEP_SIZE = 0.3

bf16 = jnp.bfloat16
f32 = jnp.float32
VMEM = pl.BlockSpec(memory_space=pltpu.VMEM)
SMEM = pl.BlockSpec(memory_space=pltpu.SMEM)


def tables():
    index = np.arange(NGRID)
    angles = 2.0 * np.pi * (index[:, None] * index[None, :] % NGRID) / NGRID
    table = np.cos(angles) + np.sin(angles)
    high = table.astype(ml_dtypes.bfloat16)
    low = (table - high.astype(np.float64)).astype(ml_dtypes.bfloat16)

    def twice(block):
        both = np.zeros((2 * NGRID, 2 * NGRID), ml_dtypes.bfloat16)
        both[:NGRID, :NGRID] = block
        both[NGRID:, NGRID:] = block
        return both

    def stacked(high, low):
        return np.concatenate([high, high, low, np.zeros_like(low)], 1)

    row = np.concatenate([twice(high), twice(low)], 1)
    order = np.concatenate([index[0::2], index[1::2]])
    parts = [row, row, stacked(high, low), stacked(high[:, order], low[:, order])]
    return np.concatenate(parts + [stacked(high[order], low[order])], 0)


def halves(value):
    high = value.astype(bf16)
    return high, (value - high.astype(f32)).astype(bf16)


def dot(left, right):
    return jnp.dot(left, right, preferred_element_type=f32)


def along_lanes(value, table):
    out = dot(jnp.concatenate(halves(value), 1), table)
    return out[:, :LANES] + out[:, LANES:]


def along_rows(value, table):
    high, low = halves(value)
    return dot(table, jnp.concatenate([high, low, high], 0))


def beside(blocks):
    return jnp.concatenate(blocks, 1)


def apart(value):
    return [value[:, i : i + LANES] for i in range(0, value.shape[1], LANES)]


def in_order(leading, pieces):
    if len(pieces) == 1:
        return pieces[0][...]
    own, other = pieces[0][...], pieces[1][...]
    return jnp.concatenate([jnp.where(leading, own, other), jnp.where(leading, other, own)], 0)


def split_table(table_ref):
    along_z = table_ref[: 4 * NGRID, :]
    rest = [table_ref[(4 + i) * NGRID : (5 + i) * NGRID, : 3 * NGRID] for i in range(3)]
    return along_z, *rest


def first_half():
    return lax.broadcasted_iota(jnp.int32, (1, LANES), 1) < NGRID


def woven(first, a, b):
    return jnp.where(first, a, pltpu.roll(b, NGRID, 1)), jnp.where(first, pltpu.roll(a, NGRID, 1), b)


def wave(k):
    return min(k, NGRID - k) * (2.0 * np.pi / BOX_LENGTH)


def kernel_base():
    def squared(k):
        line = jnp.minimum(k, NGRID - k).astype(f32) * (2.0 * np.pi / BOX_LENGTH)
        return line * line

    cube = (NGRID, LANES)
    return (
        squared(lax.broadcasted_iota(jnp.int32, cube, 0))
        + squared(lax.broadcasted_iota(jnp.int32, cube, 1) % NGRID)
        + SCREEN_SQ
    )


def forward_zy(first, pa, pb, along_z, along_y, s_ref):
    slabs = pa.shape[0] // SLAB
    even, odd = woven(first, pa, pb)
    v = jnp.concatenate([even.reshape(slabs, SLAB, LANES), odd.reshape(slabs, SLAB, LANES)], 1)
    v = along_lanes(v.reshape(slabs * NGRID, LANES), along_z).reshape(slabs, NGRID, LANES)
    v = along_rows(beside([v[i] for i in range(slabs)]), along_y)
    for i, block in enumerate(apart(v)):
        s_ref[i * NGRID : (i + 1) * NGRID, :] = block


def backward_yz(first, start, count, step, along_y, along_z, s_ref):
    v = beside([s_ref[pl.ds(start + i, NGRID, stride=step), :] for i in range(count)])
    v = jnp.concatenate(apart(along_rows(v, along_y)), 0)
    v = along_lanes(v, along_z).reshape(count, NGRID, LANES)
    return woven(first, v[:, :SLAB].reshape(count * SLAB, LANES), v[:, SLAB:].reshape(count * SLAB, LANES))


def pair_kernel(counts, n_acc, cut, n_grp, n_orb, flag_ref, group_ref, earlier_ref, table_ref, t_ref, *refs):
    refs = list(refs)
    groups = [[refs.pop(0) for _ in range(count)] for count in counts]
    acc_refs = [refs.pop(0) for _ in range(n_acc)]
    out_ref, token_ref, s_ref, s2_ref, kept_ref, out_buf, out_sems = refs[:7]
    acc_bufs, acc_sems = refs[7:-1], refs[-1]
    token_ref[...] = earlier_ref[:8, :]
    loads = [
        pltpu.make_async_copy(ref, buf, acc_sems.at[i])
        for i, (ref, buf) in enumerate(zip(acc_refs, acc_bufs))
    ]
    for load in loads:
        load.start()
    first = first_half()
    leading = group_ref[0] == 0
    along_z, along_x, along_y, back_y = split_table(table_ref)

    def fields():
        b = in_order(leading, groups[1])
        if len(groups) == 3:
            b = jnp.where(flag_ref[0] > 0, b, in_order(leading, groups[2]))
        return in_order(leading, groups[0]), b

    t = t_ref[...]
    a, b = fields()
    kept_ref[0], kept_ref[1] = a, b
    forward_zy(first, t * a, t * b, along_z, along_y, s_ref)

    base = kernel_base()
    kernels = {}
    for y in range(NGRID // 2 + 1):
        kernels[y] = (4.0 * np.pi / CELLS) / (base + wave(y) * wave(y))
    v = beside([s_ref[pl.ds(y, NGRID, stride=NGRID), :] for y in range(NGRID)])
    v = along_rows(v, along_x) * beside([kernels[min(y, NGRID - y)] for y in range(NGRID)])
    for y, block in enumerate(apart(along_rows(v, along_x))):
        s2_ref[y * NGRID : (y + 1) * NGRID, :] = block

    for load in loads:
        load.wait()
    stores = []
    for c in range(NGRID // GROUP):
        rows = slice(c * GROUP * SLAB, (c + 1) * GROUP * SLAB)
        sa, sb = backward_yz(first, c * GROUP, GROUP, NGRID, back_y, along_z, s2_ref)
        added = -(kept_ref[0, rows, :] * sa + kept_ref[1, rows, :] * sb)
        for buf in acc_bufs:
            added = added + buf[rows, :]
        if cut:
            part = ROWS // (n_grp * n_orb)
            count = n_orb * GROUP // NGRID
            pieces = added.reshape(count, n_grp, part, LANES)
            for g in range(n_grp):
                start = (g * n_orb + c * count) * part
                out_ref[start : start + count * part, :] = pieces[:, g].reshape(count * part, LANES)
        else:
            out_buf[rows, :] = added
            stores.append(pltpu.make_async_copy(out_buf.at[rows], out_ref.at[rows], out_sems.at[c]))
            stores[-1].start()
    for store in stores:
        store.wait()


def single_kernel(
    group_ref, earlier_ref, table_ref, t_ref, own_ref, other_ref, out_ref, token_ref, s_ref, s2_ref, out_buf, out_sems
):
    token_ref[...] = earlier_ref[:8, :]
    first = first_half()
    leading = group_ref[0] == 0
    along_z, along_x, along_y, back_y = split_table(table_ref)
    middle = NGRID // 2

    def both():
        own, other = own_ref[...], other_ref[...]
        return jnp.where(leading, own, other), jnp.where(leading, other, own)

    low, high = both()
    forward_zy(first, t_ref[:HALF, :] * low, t_ref[HALF:, :] * high, along_z, along_y, s_ref)

    base = kernel_base()
    ys = [(0, middle)] + [(y, NGRID - y) for y in range(1, middle)]
    kernel, blocks = [], []
    for y, z in ys:
        square = wave(y) * wave(y)
        if wave(y) != wave(z):
            square = jnp.where(first, square, wave(z) * wave(z))
        kernel.append((4.0 * np.pi / CELLS) / (base + square))
        top, bottom = woven(
            first, s_ref[pl.ds(y, middle, stride=NGRID), :], s_ref[pl.ds(z, middle, stride=NGRID), :]
        )
        blocks.append(jnp.concatenate([top, bottom], 0))
    v = along_rows(along_rows(beside(blocks), along_x) * beside(kernel), along_x)
    for (y, z), block in zip(ys, apart(v)):
        at_y, at_z = woven(first, block[:middle], block[middle:])
        s2_ref[y * middle : (y + 1) * middle, :] = at_y
        s2_ref[z * middle : (z + 1) * middle, :] = at_z

    low, high = both()
    sa, sb = backward_yz(first, 0, middle, middle, back_y, along_z, s2_ref)
    stores = []
    for c, value in enumerate((-(low * sa), -(high * sb))):
        rows = slice(c * HALF, (c + 1) * HALF)
        out_buf[rows, :] = value
        stores.append(pltpu.make_async_copy(out_buf.at[rows], out_ref.at[rows], out_sems.at[c]))
        stores[-1].start()
    for store in stores:
        store.wait()


ANY = pl.BlockSpec(memory_space=pl.ANY)
TOKEN = jax.ShapeDtypeStruct((8, LANES), f32)
FIELD = pltpu.HBM((ROWS, LANES), f32)


def pair_step(flag, group, token, target, fields, accs, cut, n_grp, n_orb):
    operands = [token, jnp.asarray(tables()), target] + [piece for field in fields for piece in field]
    counts = tuple(len(field) for field in fields)
    held = [pltpu.with_memory_space_constraint(acc, pltpu.HBM) for acc in accs]
    return pl.pallas_call(
        functools.partial(pair_kernel, counts, len(accs), cut, n_grp, n_orb),
        out_shape=(jax.ShapeDtypeStruct((ROWS, LANES), f32) if cut else FIELD, TOKEN),
        in_specs=[SMEM] * 2 + [VMEM] * len(operands) + [ANY] * len(accs),
        out_specs=(VMEM if cut else ANY, VMEM),
        scratch_shapes=[pltpu.VMEM((NGRID * NGRID, LANES), f32)] * 2
        + [pltpu.VMEM((2, ROWS, LANES), f32)]
        + [pltpu.VMEM((ROWS, LANES), f32), pltpu.SemaphoreType.DMA((2,))]
        + [pltpu.VMEM((ROWS, LANES), f32)] * len(accs)
        + [pltpu.SemaphoreType.DMA((max(len(accs), 1),))],
        compiler_params=pltpu.CompilerParams(vmem_limit_bytes=44 << 20),
        cost_estimate=pl.CostEstimate(flops=10**8 if cut else 8 * 10**9, bytes_accessed=1 << 18, transcendentals=0),
    )(flag.reshape(1), group.reshape(1), *operands, *held)


def single_step(group, token, target, pieces):
    return pl.pallas_call(
        single_kernel,
        out_shape=(FIELD, TOKEN),
        in_specs=[SMEM] + [VMEM] * 5,
        out_specs=(ANY, VMEM),
        scratch_shapes=[pltpu.VMEM((NGRID * NGRID // 2, LANES), f32)] * 2
        + [pltpu.VMEM((ROWS, LANES), f32), pltpu.SemaphoreType.DMA((2,))],
        compiler_params=pltpu.CompilerParams(vmem_limit_bytes=40 << 20),
        cost_estimate=pl.CostEstimate(flops=10**10, bytes_accessed=4 << 20, transcendentals=0),
    )(group.reshape(1), token, jnp.asarray(tables()), target, *pieces)


def strided(ref, r, count, step):
    return ref[pl.ds(r, count, stride=step), :]


def gram_kernel(n, part, place_ref, x_ref, tl_ref, tu_ref, th_ref, v_ref, out_ref, t_ref):
    group = place_ref[0]
    x = beside([strided(x_ref, r, n, part) for r in range(part)])
    rows = th_ref.shape[0] // part
    low = beside([strided(tl_ref, r, rows, part) for r in range(part)])
    high = beside([strided(tu_ref, r, rows, part) for r in range(part)])
    own = jnp.where(group == 0, low, high)
    other = beside([strided(th_ref, r, rows, part) for r in range(part)])
    t = jnp.concatenate([jnp.where(group == 0, own, other), jnp.where(group == 0, other, own)], 0)
    t_ref[...] = t
    v = beside([v_ref[r : r + 1, :] for r in range(part)])
    xh, xl = halves(x)
    th, tl = halves(t)
    wh, wl = halves(t * v)
    left = jnp.concatenate([xh, th, xl, tl], 0)
    right = jnp.concatenate([xh, th, wh, xl, tl, wl], 0)
    full = lax.dot_general(left, right, (((1,), (1,)), ((), ())), preferred_element_type=f32)
    full = full[: 2 * n] + full[2 * n :]
    full = full[:, : 3 * n] + full[:, 3 * n :]
    out_ref[...] = jnp.concatenate([full[:n, : 2 * n], full[n:, 2 * n :]], 1) * (1.0 / CELLS)


def gram_step(group, x, tl, tu, th, v, n, part):
    return pl.pallas_call(
        functools.partial(gram_kernel, n, part),
        out_shape=(
            jax.ShapeDtypeStruct((n, 3 * n), f32),
            jax.ShapeDtypeStruct((n, part * LANES), f32),
        ),
        in_specs=[SMEM] + [VMEM] * 5,
        out_specs=(VMEM, VMEM),
        compiler_params=pltpu.CompilerParams(vmem_limit_bytes=32 << 20),
        cost_estimate=pl.CostEstimate(flops=10**9, bytes_accessed=2 << 20, transcendentals=0),
    )(group.reshape(1), x, tl, tu, th, v)


def exact(left, right, dims):
    return lax.dot_general(
        left, right, (dims, ((), ())), precision=lax.Precision.HIGHEST, preferred_element_type=f32
    )


def mixed_rows(n, part, out_rows, first, mix, x_ref, t_ref, v_ref):
    x = beside([strided(x_ref, r, n, part) for r in range(part)])
    t = t_ref[...]
    own = t_ref[pl.ds(first, out_rows), :]
    v = beside([v_ref[r : r + 1] for r in range(part)])
    xh, xl = halves(x)
    th, tl = halves(t)
    both = dot(mix, jnp.concatenate([xh, th, xl, tl], 0))
    return own * (1.0 - STEP_SIZE * v) + both[:out_rows] + both[out_rows:]


def eliminated(work, n):
    ids = lax.broadcasted_iota(jnp.int32, (8, 1), 0)
    blocks = [work[i : i + 8] for i in range(0, n, 8)]
    for k in range(n):
        at, inside = divmod(k, 8)
        row = blocks[at][inside : inside + 1]
        root = lax.rsqrt(row[:, k : k + 1])
        row = row * root
        for i in range(at, len(blocks)):
            column = blocks[i][:, k : k + 1] * root
            if i > at:
                blocks[i] = blocks[i] - column * row
            else:
                lower = blocks[i] - jnp.where(ids > inside, column, 0.0) * row
                blocks[i] = jnp.where(ids == inside, row, lower)
    return jnp.concatenate(blocks, 0)


def partner_kernel(n, part, out_rows, place_ref, g_ref, x_ref, t_ref, v_ref, out_ref, mix_ref, m_ref, r_ref):
    group = place_ref[0]
    ids = lax.broadcasted_iota(jnp.int32, (n, 1), 0)
    columns = lax.broadcasted_iota(jnp.int32, (1, 3 * n), 1)
    eye = (lax.broadcasted_iota(jnp.int32, (n, n), 0) == lax.broadcasted_iota(jnp.int32, (n, n), 1)).astype(f32)
    work = jnp.concatenate([g_ref[:, : 2 * n], eye], 1)

    def eliminate(k, work):
        row = jnp.sum(jnp.where(ids == k, work, 0.0), axis=0, keepdims=True)
        pivot = jnp.sum(jnp.where(columns == k, row, 0.0), axis=1, keepdims=True)
        column = jnp.sum(jnp.where(columns == k, work, 0.0), axis=1, keepdims=True)
        root = lax.rsqrt(pivot)
        row = row * root
        lower = work - jnp.where(ids > k, column * root, 0.0) * row
        return jnp.where(ids == k, row, lower)

    work = eliminated(work, n) if n <= 32 else lax.fori_loop(0, n, eliminate, work)
    pt = work[:, n : 2 * n]
    m_ref[...] = exact(pt, work[:, 2 * n :], ((0,), (0,)))
    r_ref[...] = g_ref[:, 2 * n :] - exact(pt, pt, ((0,), (0,)))

    def mixer(start):
        rows = pl.ds(start, out_rows)
        mix = jnp.concatenate([m_ref[rows, :], r_ref[rows, :]], 1) * STEP_SIZE
        high, low = halves(mix)
        return jnp.concatenate([jnp.concatenate([high, high], 1), jnp.concatenate([low, low], 1)], 0)

    mix_ref[...] = mixer(pl.multiple_of(group * out_rows, 8))
    first = pl.multiple_of((1 - group) * out_rows, 8)
    out_ref[...] = mixed_rows(n, part, out_rows, first, mixer(first), x_ref, t_ref, v_ref)


def partner_step(group, g, x, t, v, n, part, out_rows):
    return pl.pallas_call(
        functools.partial(partner_kernel, n, part, out_rows),
        out_shape=(
            jax.ShapeDtypeStruct((out_rows, part * LANES), f32),
            jax.ShapeDtypeStruct((2 * out_rows, 4 * n), bf16),
        ),
        in_specs=[SMEM] + [VMEM] * 4,
        out_specs=(VMEM, VMEM),
        scratch_shapes=[pltpu.VMEM((n, n), f32)] * 2,
        compiler_params=pltpu.CompilerParams(vmem_limit_bytes=32 << 20),
        cost_estimate=pl.CostEstimate(flops=4 * 10**9, bytes_accessed=2 << 20, transcendentals=0),
    )(group.reshape(1), g, x, t, v)


def own_kernel(n, part, out_rows, place_ref, mix_ref, x_ref, t_ref, v_ref, out_ref):
    group = place_ref[0]
    width = part * LANES
    first = pl.multiple_of(group * out_rows, 8)
    out_ref[:, pl.ds(pl.multiple_of(group * width, width), width)] = mixed_rows(
        n, part, out_rows, first, mix_ref[...], x_ref, t_ref, v_ref
    )


def own_step(group, mix, x, t, v, n, part, out_rows):
    return pl.pallas_call(
        functools.partial(own_kernel, n, part, out_rows),
        out_shape=jax.ShapeDtypeStruct((out_rows, 2 * part * LANES), f32),
        in_specs=[SMEM] + [VMEM] * 4,
        out_specs=VMEM,
        compiler_params=pltpu.CompilerParams(vmem_limit_bytes=32 << 20),
        cost_estimate=pl.CostEstimate(flops=4 * 10**9, bytes_accessed=2 << 20, transcendentals=0),
    )(group.reshape(1), mix, x, t, v)


def moved(x, axes, target):
    size = 1
    for axis in axes:
        size *= lax.axis_size(axis)
    return lax.ppermute(x, axes, [(i, target(i)) for i in range(size)])


def summed_over(x, bits):
    masks = bits if len(bits) == 1 else [bits[0], bits[1], bits[0] ^ bits[1]]
    parts = [moved(x, ("grp", "orb"), lambda i, m=m: i ^ m) for m in masks]
    for part in parts:
        x = x + part
    return x


def on_device(occupied, targets, potential):
    n_grp, n_orb = lax.axis_size("grp"), lax.axis_size("orb")
    n = n_grp * n_orb
    part = ROWS // n
    group, orb = lax.axis_index("grp"), lax.axis_index("orb")
    one = jnp.ones((), f32)
    crossed = (((orb >> 1) & 1) != (orb & 1)).astype(f32)

    def spread(value):
        return lax.all_to_all(value.reshape(n, part, LANES), ("grp", "orb"), split_axis=0, concat_axis=0).reshape(ROWS, LANES)

    def swapped(value):
        return moved(value, ("grp",), lambda i: i ^ 1)

    def mates(pieces):
        return [moved(v, ("orb",), lambda i: i ^ 1) for v in pieces]

    target = targets.reshape(ROWS, LANES)
    own = occupied.reshape(ROWS, LANES)
    mine = lax.dynamic_slice_in_dim(own, group * (ROWS // 2), ROWS // 2, 0)
    near = moved(mine, ("orb",), lambda i: i ^ 2)
    mate = mates([own])

    def owned(value, start):
        piece = value.reshape(n_orb, n_grp * part, LANES)[:, start : start + part]
        return lax.all_to_all(piece, ("orb",), split_axis=0, concat_axis=0).reshape(HALF, LANES)

    t_low = owned(target, 0)
    near, token = lax.optimization_barrier((near, potential.reshape(-1, LANES)))
    begun, token = pair_step(one, group, token, target, [[own], mate], [], False, n_grp, n_orb)
    far = moved(near, ("orb",), lambda i: (i + (-4 if i & 2 else 4)) % n_orb)
    near = [near, swapped(near)]
    far, near, late, token, t_low = lax.optimization_barrier((far, near, target, token, t_low))
    far_mate = mates([far])
    far = [far, swapped(far)]
    near_mate = mates(near)
    t_high = owned(late, part)
    going, token = single_step(group, token, target, near)
    far, token = lax.optimization_barrier((far, token))
    fields = [far, near_mate, far_mate + mates(far[1:])]
    acc, token = pair_step(crossed, group, token, target, fields, [begun, going], True, n_grp, n_orb)
    acc, t_low, t_high = lax.optimization_barrier((acc, t_low, t_high))
    t_other = swapped(jnp.where(group == 0, t_high, t_low))
    x_half = spread(acc)

    v = lax.dynamic_slice_in_dim(potential.reshape(n_grp * part, LANES), group * part, part, 0)
    gram, t_half = gram_step(group, x_half, t_low, t_high, t_other, v, n, part)
    rest = [b for b in (1 << k for k in range(2, 30)) if b < n_orb]
    for step in [[1]] + [rest[k : k + 2] for k in range(0, len(rest), 2)] + [[2, n_orb]]:
        gram = summed_over(gram, step)
    partner, mix = partner_step(group, gram, x_half, t_half, v, n, part, n_orb)
    update = own_step(group, mix, x_half, t_half, v, n, part, n_orb)
    width = part * LANES
    return lax.dynamic_update_slice(update, swapped(partner), (0, (1 - group) * width))


def solution(mesh):
    placed = (P("orb", None), P(("grp", "orb"), None), P("orb"))
    return jax.shard_map(
        on_device, mesh=mesh, in_specs=placed, out_specs=P("grp", "orb"), check_vma=False
    )
```
